256 devices in a mesh: gx: 4 (over x), gy: 8 (over y, core), gz: 8 (over z).
Axes of the slice: x: 4, y: 4, z: 8, core: 2. Of those that a mesh axis runs over, the one named last changes fastest.
Arguments:
- conserved: float32 [5, 64, 128, 1024], P(None, 'gx', 'gy', 'gz'), may hold values from -20 to 80, as said below
- potential: float32 [64, 128, 1024], P('gx', 'gy', 'gz'), may hold values from -12 to 12
Outputs:
- updated: float32 [5, 64, 128, 1024], P(None, 'gx', 'gy', 'gz')
- potential_out: float32 [64, 128, 1024], P('gx', 'gy', 'gz')
The draws below stay inside these ranges and needn't reach their ends.
Inputs may be any that keep to these rules, and one draw needn't show every extreme that they name: `conserved`: channel 0 is a positive density, channels 1 to 3 the momentum and channel 4 the total energy; the pressure computed from them is positive in every cell.
All inputs are finite; a program needn't handle non-finite values.
Results may differ from the reference program's by a relative error of at most 0.0003.
Values sent between devices are 32-bit elements; how exact they have to be, the bound alone decides.
No kernel may reach another device: no remote copies, remote signals or barrier semaphores. Data moves between devices by JAX's collectives and lax.ppermute only.
A program may use at most 64 MiB of HBM per device.

```python
import math
import jax
import jax.numpy as jnp
from jax import lax

LEVELS = 3
NX = 64
NY = 128
NZ = 1024


def draw_conserved(key, part):
    key = jax.random.fold_in(key, 7)
    key_density, key_velocity, key_heat = jax.random.split(key, 3)
    shape = (NX, NY, NZ)
    position_x = jnp.arange(NX).astype(jnp.float32)
    fraction_x = (position_x / float(NX) - 0.5)[:, None, None]
    log_density = jax.random.uniform(key_density, shape, jnp.float32, -1.0, 0.7) + math.log(3.0) * fraction_x
    velocity = jnp.clip(0.8 * jax.random.normal(key_velocity, (3,) + shape, jnp.float32), -3.0, 3.0)
    heat = jax.random.uniform(key_heat, shape, jnp.float32, 0.6, 1.5)
    density = jnp.exp(log_density)
    pressure = density * heat
    momentum = density[None] * velocity
    energy = pressure * 1.5 + 0.5 * density * (velocity[0] * velocity[0] + velocity[1] * velocity[1] + velocity[2] * velocity[2])
    return jnp.concatenate([density[None], momentum, energy[None]], 0)


def block_levels(rng, extent, shards, least, largest):
    level = 1.0
    for position, blocks in shards:
        heights = jax.random.uniform(jax.random.fold_in(jax.random.fold_in(rng, 6), position), (blocks,), jnp.float32, least / len(shards), largest / len(shards))
        level = level * jnp.repeat(jnp.exp(heights), extent[position] // blocks).reshape((-1,) + (1,) * (len(extent) - 1 - position))
    return level


def centred(own_key, shape, spread, limit, shards=(), held_as=jnp.bfloat16):
    values = jax.random.normal(own_key, shape, jnp.float32) * spread
    if len(shards) > 0:
        values = block_levels(own_key, shape, shards, -0.22, 0.18) * values
    return jnp.clip(values, min=-limit, max=limit).astype(held_as)


def setup_inputs(seed: int = 0) -> dict:
    streams_of = jax.random.split(jax.random.key(seed), 3)
    conserved = draw_conserved(jax.random.fold_in(streams_of[2], 71), 0)
    potential = centred(streams_of[1], (NX, NY, NZ), 2.0, 12.0, ((0, 4), (1, 8), (2, 8)), jnp.float32)
    return dict(conserved=conserved, potential=potential)


gamma_gas = 5.0 / 3.0
courant = 0.4
coupling = 0.01

def primitives(conserved):
    density = conserved[0]
    velocity = conserved[1:4] / density
    kinetic = 0.5 * density * (velocity[0] * velocity[0] + velocity[1] * velocity[1] + velocity[2] * velocity[2])
    pressure = (gamma_gas - 1.0) * (conserved[4] - kinetic)
    return jnp.concatenate([density[None], velocity, pressure[None]], 0)

def limited(first, second):
    return 0.5 * (jnp.sign(first) + jnp.sign(second)) * jnp.minimum(jnp.abs(first), jnp.abs(second))

def hllc(left_state, right_state, normal):
    others = ((1, 2), (0, 2), (0, 1))[normal]

    def unpack(primitive):
        density = primitive[0]
        normal_speed = primitive[1 + normal]
        trans_one = primitive[1 + others[0]]
        trans_two = primitive[1 + others[1]]
        pressure = primitive[4]
        energy = pressure / (gamma_gas - 1.0) + 0.5 * density * (normal_speed * normal_speed + trans_one * trans_one + trans_two * trans_two)
        sound_speed = jnp.sqrt(gamma_gas * pressure / density)
        return (density, normal_speed, trans_one, trans_two, pressure, energy, sound_speed)
    left_terms = unpack(left_state)
    right_terms = unpack(right_state)
    low_wave = jnp.minimum(left_terms[1] - left_terms[6], right_terms[1] - right_terms[6])
    high_wave = jnp.maximum(left_terms[1] + left_terms[6], right_terms[1] + right_terms[6])
    left_mass = left_terms[0] * (low_wave - left_terms[1])
    right_mass = right_terms[0] * (high_wave - right_terms[1])
    star_wave = (right_terms[4] - left_terms[4] + left_mass * left_terms[1] - right_mass * right_terms[1]) / (left_mass - right_mass)

    def fluxes(quantities, wave_speed, mass_rate):
        density, normal_speed, trans_one, trans_two, pressure, energy, sound_speed = quantities
        direct = [density * normal_speed, density * normal_speed * normal_speed + pressure, density * normal_speed * trans_one, density * normal_speed * trans_two, normal_speed * (energy + pressure)]
        stored = [density, density * normal_speed, density * trans_one, density * trans_two, energy]
        factor = mass_rate / (wave_speed - star_wave)
        starred = [factor, factor * star_wave, factor * trans_one, factor * trans_two, factor * (energy / density + (star_wave - normal_speed) * (star_wave + pressure / mass_rate))]
        return (direct, [direct[member] + wave_speed * (starred[member] - stored[member]) for member in range(5)])
    left_direct, left_star = fluxes(left_terms, low_wave, left_mass)
    right_direct, right_star = fluxes(right_terms, high_wave, right_mass)
    chosen = [jnp.where(low_wave >= 0.0, left_direct[member], jnp.where(star_wave >= 0.0, left_star[member], jnp.where(high_wave > 0.0, right_star[member], right_direct[member]))) for member in range(5)]
    momentum = [None, None, None]
    momentum[normal] = chosen[1]
    momentum[others[0]] = chosen[2]
    momentum[others[1]] = chosen[3]
    return jnp.stack([chosen[0]] + momentum + [chosen[4]], 0)

def face_flux(before, centre, after_one, after_two, normal):
    left_state = centre + 0.5 * limited(centre - before, after_one - centre)
    right_state = after_one - 0.5 * limited(after_one - centre, after_two - after_one)
    return hllc(left_state, right_state, normal)

def neighbours(values_in):
    total_sum = jnp.roll(values_in, -1, 0) + jnp.roll(values_in, 1, 0)
    total_sum = total_sum + jnp.roll(values_in, -1, 1) + jnp.roll(values_in, 1, 1)
    total_sum = total_sum + jnp.roll(values_in, -1, 2) + jnp.roll(values_in, 1, 2)
    return total_sum

def parity_of(shape):
    summed = lax.broadcasted_iota(jnp.int32, shape, 0) + lax.broadcasted_iota(jnp.int32, shape, 1) + lax.broadcasted_iota(jnp.int32, shape, 2)
    return summed % 2

def sweep(values_in, source, spacing_sq):
    parity = parity_of(values_in.shape)
    for colour in (0, 1):
        renewed = (neighbours(values_in) - spacing_sq * source) / 6.0
        values_in = jnp.where(parity == colour, renewed, values_in)
    return values_in

def coarsen(values_in):
    first, second, third = values_in.shape
    return lax.optimization_barrier(jnp.mean(values_in.reshape(first // 2, 2, second // 2, 2, third // 2, 2), axis=(1, 3, 5)))

def refine(values_in):
    return jnp.repeat(jnp.repeat(jnp.repeat(values_in, 2, 0), 2, 1), 2, 2)

def eigenvalues(shape, spacing_sq):
    result = jnp.zeros(shape, jnp.float32)
    zero_mode = jnp.ones(shape, jnp.bool_)
    for along in range(3):
        wave_index = lax.broadcasted_iota(jnp.int32, shape, along)
        angle = 2.0 * math.pi / shape[along] * wave_index.astype(jnp.float32)
        result = result + (2.0 * jnp.cos(angle) - 2.0) / spacing_sq
        zero_mode = jnp.logical_and(zero_mode, wave_index == 0)
    return (result, zero_mode)

def coarse_solve(source, spacing_sq):
    spectrum = jnp.fft.fftn(source)
    eigen_value, zero_mode = eigenvalues(source.shape, spacing_sq)
    divided = jnp.where(zero_mode, 0.0, spectrum / jnp.where(zero_mode, 1.0, eigen_value))
    return jnp.real(jnp.fft.ifftn(divided)).astype(source.dtype)

def vcycle(values_in, source, depth_now):
    spacing_sq = float(4 ** depth_now)
    if depth_now == LEVELS:
        return coarse_solve(source, spacing_sq)
    values_in = sweep(values_in, source, spacing_sq)
    defect = source - (neighbours(values_in) - 6.0 * values_in) / spacing_sq
    coarse_source = coarsen(defect)
    correction = vcycle(jnp.zeros_like(coarse_source), coarse_source, depth_now + 1)
    values_in = values_in + refine(correction)
    return sweep(values_in, source, spacing_sq)

def reference(conserved, potential):
    density = conserved[0]
    mean_density = jnp.sum(density) / float(NX * NY * NZ)
    gravity_source = coupling * (density - mean_density)
    potential_out = vcycle(potential, gravity_source, 0)
    primitive = primitives(conserved)
    sound_speed = jnp.sqrt(gamma_gas * primitive[4] / primitive[0])
    signal = jnp.abs(primitive[1]) + sound_speed + (jnp.abs(primitive[2]) + sound_speed) + (jnp.abs(primitive[3]) + sound_speed)
    step_size = courant / jnp.max(signal)
    update = jnp.zeros_like(conserved)
    for normal in range(3):
        array_axis = 1 + normal
        fluxes = face_flux(jnp.roll(primitive, 1, array_axis), primitive, jnp.roll(primitive, -1, array_axis), jnp.roll(primitive, -2, array_axis), normal)
        update = update - (fluxes - jnp.roll(fluxes, 1, array_axis))
    gradients = [(jnp.roll(potential_out, -1, along) - jnp.roll(potential_out, 1, along)) * 0.5 for along in range(3)]
    energy_source = -(conserved[1] * gradients[0] + conserved[2] * gradients[1] + conserved[3] * gradients[2])
    source_terms = jnp.stack([jnp.zeros_like(density), -density * gradients[0], -density * gradients[1], -density * gradients[2], energy_source], 0)
    updated = conserved + step_size * (update + source_terms)
    return (updated, potential_out)
```

```python
import math

import numpy as np
import jax
import jax.numpy as jnp
from jax import lax
from jax.sharding import PartitionSpec as P

LEVELS = 3


gamma_gas = 5.0 / 3.0
courant = 0.4
coupling = 0.01


def primitives(conserved):
    density = conserved[0]
    velocity = conserved[1:4] / density
    kinetic = (
        0.5
        * density
        * (velocity[0] * velocity[0] + velocity[1] * velocity[1] + velocity[2] * velocity[2])
    )
    pressure = (gamma_gas - 1.0) * (conserved[4] - kinetic)
    return jnp.concatenate([density[None], velocity, pressure[None]], 0)


def limited(first, second):
    return 0.5 * (jnp.sign(first) + jnp.sign(second)) * jnp.minimum(jnp.abs(first), jnp.abs(second))


def hllc(left_state, right_state, normal):
    others = ((1, 2), (0, 2), (0, 1))[normal]

    def unpack(primitive):
        density = primitive[0]
        normal_speed = primitive[1 + normal]
        trans_one = primitive[1 + others[0]]
        trans_two = primitive[1 + others[1]]
        pressure = primitive[4]
        energy = pressure / (gamma_gas - 1.0) + 0.5 * density * (
            normal_speed * normal_speed + trans_one * trans_one + trans_two * trans_two
        )
        sound_speed = jnp.sqrt(gamma_gas * pressure / density)
        return (density, normal_speed, trans_one, trans_two, pressure, energy, sound_speed)

    left_terms = unpack(left_state)
    right_terms = unpack(right_state)
    low_wave = jnp.minimum(left_terms[1] - left_terms[6], right_terms[1] - right_terms[6])
    high_wave = jnp.maximum(left_terms[1] + left_terms[6], right_terms[1] + right_terms[6])
    left_mass = left_terms[0] * (low_wave - left_terms[1])
    right_mass = right_terms[0] * (high_wave - right_terms[1])
    star_wave = (
        right_terms[4] - left_terms[4] + left_mass * left_terms[1] - right_mass * right_terms[1]
    ) / (left_mass - right_mass)

    def fluxes(quantities, wave_speed, mass_rate):
        density, normal_speed, trans_one, trans_two, pressure, energy, sound_speed = quantities
        direct = [
            density * normal_speed,
            density * normal_speed * normal_speed + pressure,
            density * normal_speed * trans_one,
            density * normal_speed * trans_two,
            normal_speed * (energy + pressure),
        ]
        stored = [density, density * normal_speed, density * trans_one, density * trans_two, energy]
        factor = mass_rate / (wave_speed - star_wave)
        starred = [
            factor,
            factor * star_wave,
            factor * trans_one,
            factor * trans_two,
            factor
            * (energy / density + (star_wave - normal_speed) * (star_wave + pressure / mass_rate)),
        ]
        return (
            direct,
            [
                direct[member] + wave_speed * (starred[member] - stored[member])
                for member in range(5)
            ],
        )

    left_direct, left_star = fluxes(left_terms, low_wave, left_mass)
    right_direct, right_star = fluxes(right_terms, high_wave, right_mass)
    chosen = [
        jnp.where(
            low_wave >= 0.0,
            left_direct[member],
            jnp.where(
                star_wave >= 0.0,
                left_star[member],
                jnp.where(high_wave > 0.0, right_star[member], right_direct[member]),
            ),
        )
        for member in range(5)
    ]
    momentum = [None, None, None]
    momentum[normal] = chosen[1]
    momentum[others[0]] = chosen[2]
    momentum[others[1]] = chosen[3]
    return jnp.stack([chosen[0]] + momentum + [chosen[4]], 0)


def face_flux(before, centre, after_one, after_two, normal):
    left_state = centre + 0.5 * limited(centre - before, after_one - centre)
    right_state = after_one - 0.5 * limited(after_one - centre, after_two - after_one)
    return hllc(left_state, right_state, normal)

AXES = ("gx", "gy", "gz")
EXACT = lax.Precision.HIGHEST


def shift(payload, axis, step):
    count = lax.axis_size(axis)
    return lax.ppermute(payload, axis, [(i, (i + step) % count) for i in range(count)])


def exchange(head, tail, axis):
    return shift(tail, axis, 1), shift(head, axis, -1)


def inner(cells, width=1):
    return cells[width:-width, width:-width, width:-width]


def stencil_sum(padded):
    total_sum = padded[2:, 1:-1, 1:-1] + padded[:-2, 1:-1, 1:-1]
    total_sum = total_sum + padded[1:-1, 2:, 1:-1] + padded[1:-1, :-2, 1:-1]
    total_sum = total_sum + padded[1:-1, 1:-1, 2:] + padded[1:-1, 1:-1, :-2]
    return total_sum


def parity_of(shape, origin):
    summed = (
        lax.broadcasted_iota(jnp.int32, shape, 0)
        + lax.broadcasted_iota(jnp.int32, shape, 1)
        + lax.broadcasted_iota(jnp.int32, shape, 2)
    )
    return (summed + 3 * abs(origin)) % 2


def half_sweep(values_in, source, spacing_sq, colour, origin):
    renewed = (stencil_sum(values_in) - spacing_sq * source) / 6.0
    return jnp.where(parity_of(source.shape, origin) == colour, renewed, inner(values_in))


def coarsen(cells):
    first, second, third = cells.shape
    pairs = cells.reshape(first // 2, 2, second // 2, 2, third).sum(axis=(1, 3))
    table = np.repeat(np.eye(third // 2, dtype=np.float32), 2, 0) * 0.125
    return jnp.dot(pairs.reshape(-1, third), table, precision=EXACT).reshape(first // 2, second // 2, third // 2)


def refine(cells):
    first, second, third = cells.shape
    table = np.repeat(np.eye(third, dtype=np.float32), 2, 1)
    wide = jnp.dot(cells.reshape(-1, third), table, precision=EXACT).reshape(first, 1, second, 1, 2 * third)
    return jnp.broadcast_to(wide, (first, 2, second, 2, 2 * third)).reshape(2 * first, 2 * second, 2 * third)


def take_columns(cells, start, width):
    extent = cells.shape[-1]
    table = np.zeros((width, extent), np.float32)
    table[np.arange(width), start + np.arange(width)] = 1.0
    return lax.dot_general(table, cells.reshape(-1, extent), (((1,), (1,)), ((), ())), precision=EXACT)


def widen(cells, left, right):
    extent = cells.shape[-1]
    width = left.shape[0]
    sides = jnp.concatenate([left, right], 0)
    flat = lax.dot_general(sides, np.eye(2 * width, dtype=np.float32), (((0,), (0,)), ((), ())), precision=EXACT)
    flat = flat.reshape(cells.shape[:-1] + (2 * width,))
    return jnp.concatenate([flat[..., :width], cells, flat[..., width:]], -1)


def cas(extent):
    angle = 2.0 * np.pi / extent * np.outer(np.arange(extent), np.arange(extent))
    return (np.cos(angle) + np.sin(angle)) / np.sqrt(extent)


def eigen(extent, spacing_sq):
    return (2.0 * np.cos(2.0 * np.pi / extent * np.arange(extent)) - 2.0) / spacing_sq


def coarse_tables(shape, spacing_sq):
    first, second, third = (extent // 2 for extent in shape)
    plane = np.kron(cas(first), cas(second))
    line = cas(third)
    pair_plane = np.kron(np.repeat(np.eye(first), 2, 1), np.repeat(np.eye(second), 2, 1))
    pair_line = np.repeat(np.eye(third), 2, 0)
    total = (eigen(first, spacing_sq)[:, None] + eigen(second, spacing_sq)).reshape(-1, 1) + eigen(third, spacing_sq)
    total[0, 0] = 1.0
    inverse = 1.0 / total
    inverse[0, 0] = 0.0
    tables = (plane @ pair_plane / 4.0, pair_line @ line / 2.0, inverse, pair_plane.T @ plane, line @ pair_line.T)
    return tuple(table.astype(np.float32) for table in tables)


def periodic_sum(cells):
    total_sum = jnp.roll(cells, -1, 0) + jnp.roll(cells, 1, 0)
    total_sum = total_sum + jnp.roll(cells, -1, 1) + jnp.roll(cells, 1, 1)
    return total_sum + jnp.roll(cells, -1, 2) + jnp.roll(cells, 1, 2)


def global_level(source, spacing_sq):
    parity = parity_of(source.shape, 0)
    first = jnp.where(parity == 0, -spacing_sq * source / 6.0, 0.0)
    first = jnp.where(parity == 1, (periodic_sum(first) - spacing_sq * source) / 6.0, first)
    defect = source - (periodic_sum(first) - 6.0 * first) / spacing_sq
    to_plane, to_line, inverse, from_plane, from_line = coarse_tables(source.shape, 4.0 * spacing_sq)
    flat = defect.reshape(-1, source.shape[2])
    modes = jnp.dot(jnp.dot(to_plane, flat, precision=EXACT), to_line, precision=EXACT) * inverse
    correction = jnp.dot(jnp.dot(from_plane, modes, precision=EXACT), from_line, precision=EXACT)
    second = first + correction.reshape(source.shape)
    for colour in (0, 1):
        second = jnp.where(parity == colour, (periodic_sum(second) - spacing_sq * source) / 6.0, second)
    return second


def picker(fine_count, coarse_extent, start, halo):
    wanted = (start + lax.broadcasted_iota(jnp.int32, (fine_count, coarse_extent), 0) // 2 - halo) % coarse_extent
    return (wanted == lax.broadcasted_iota(jnp.int32, (fine_count, coarse_extent), 1)).astype(jnp.float32)


def shards(conserved, potential):
    density = conserved[0]
    cells_x, cells_y, cells_z = density.shape
    count_x, count_y, count_z = (lax.axis_size(axis) for axis in AXES)
    devices = count_x * count_y * count_z
    total_cells = float(cells_x * cells_y * cells_z * devices)

    left, right = exchange(
        jnp.concatenate([potential[:7], density[:6]], 0),
        jnp.concatenate([potential[-7:], density[-6:]], 0),
        "gx",
    )
    phi = jnp.concatenate([left[:7], potential, right[:7]], 0)
    rho = jnp.concatenate([left[7:], density, right[7:]], 0)
    left, right = exchange(
        jnp.concatenate([phi[:, :7].swapaxes(0, 1).reshape(-1, cells_z), rho[:, :6].swapaxes(0, 1).reshape(-1, cells_z)], 0),
        jnp.concatenate([phi[:, -7:].swapaxes(0, 1).reshape(-1, cells_z), rho[:, -6:].swapaxes(0, 1).reshape(-1, cells_z)], 0),
        "gy",
    )

    def rows(flat, width, lines):
        return flat.reshape(width, lines, cells_z).swapaxes(0, 1)

    cut = 7 * (cells_x + 14)
    phi = jnp.concatenate([rows(left[:cut], 7, cells_x + 14), phi, rows(right[:cut], 7, cells_x + 14)], 1)
    rho = jnp.concatenate([rows(left[cut:], 6, cells_x + 12), rho, rows(right[cut:], 6, cells_x + 12)], 1)
    lines_phi = phi.shape[0] * phi.shape[1]
    lines_rho = rho.shape[0] * rho.shape[1]

    def flat_ends(start_phi, start_rho):
        return jnp.concatenate(
            [take_columns(phi, start_phi, 7).reshape(-1), take_columns(rho, start_rho, 6).reshape(-1)], 0
        )

    left, right = exchange(flat_ends(0, 0), flat_ends(cells_z - 7, cells_z - 6), "gz")
    cut = 7 * lines_phi
    phi = widen(phi, left[:cut].reshape(7, lines_phi), right[:cut].reshape(7, lines_phi))
    rho = widen(rho, left[cut:].reshape(6, lines_rho), right[cut:].reshape(6, lines_rho))

    source = coupling * rho
    swept = half_sweep(phi, source, 1.0, 0, -6)
    swept = half_sweep(swept, inner(source), 1.0, 1, -5)
    source_one = coarsen(inner(source, 2) - (stencil_sum(swept) - 6.0 * inner(swept)))
    start_one = jnp.where(parity_of(source_one.shape, -2) == 0, -4.0 * source_one / 6.0, 0.0)
    swept_one = half_sweep(start_one, inner(source_one), 4.0, 1, -1)
    source_two = coarsen(inner(source_one, 2) - (stencil_sum(swept_one) - 6.0 * inner(swept_one)) / 4.0)

    primitive = primitives(conserved)
    sound_speed = jnp.sqrt(gamma_gas * primitive[4] / primitive[0])
    signal = (
        jnp.abs(primitive[1])
        + sound_speed
        + (jnp.abs(primitive[2]) + sound_speed)
        + (jnp.abs(primitive[3]) + sound_speed)
    )
    two_x, two_y, two_z = source_two.shape
    two_cells = two_x * two_y * two_z
    lane = lax.broadcasted_iota(jnp.int32, (128,), 0)
    extra = jnp.where(lane == 0, jnp.sum(density), jnp.where(lane == 1, jnp.max(signal), 0.0))
    payload = jnp.concatenate([source_two.reshape(-1), extra], 0)
    gathered = lax.all_to_all(
        jnp.broadcast_to(payload[None], (devices, payload.shape[0])), AXES, 0, 0, tiled=True
    )

    own_one = inner(source_one, 2)
    flow = conserved[1:]
    left, right = exchange(own_one[:5], own_one[-5:], "gx")
    wide_one = jnp.concatenate([left, own_one, right], 0)
    left, right = exchange(flow[:, :2], flow[:, -2:], "gx")
    flow_x = jnp.concatenate([left, flow, right], 1)
    left, right = exchange(wide_one[:, :5], wide_one[:, -5:], "gy")
    wide_one = jnp.concatenate([left, wide_one, right], 1)
    left, right = exchange(flow[:, :, :2], flow[:, :, -2:], "gy")
    flow_y = jnp.concatenate([left, flow, right], 2)
    lines_one = wide_one.shape[0] * wide_one.shape[1]

    def both_ends(start_one_col, start_flow):
        return jnp.concatenate(
            [take_columns(wide_one, start_one_col, 5).reshape(-1), take_columns(flow, start_flow, 2).reshape(-1)], 0
        )

    left, right = exchange(both_ends(0, 0), both_ends(own_one.shape[2] - 5, cells_z - 2), "gz")
    cut = 5 * lines_one
    wide_one = widen(wide_one, left[:cut].reshape(5, lines_one), right[:cut].reshape(5, lines_one))
    flow_z = widen(flow, left[cut:].reshape(2, -1), right[cut:].reshape(2, -1))

    update = jnp.zeros_like(conserved)
    for normal, flow_wide in enumerate((flow_x, flow_y, flow_z)):
        array_axis = 1 + normal
        extent = conserved.shape[array_axis]
        selector = [slice(6, -6), slice(6, -6), slice(6, -6)]
        selector[normal] = slice(4, -4)
        slab = primitives(jnp.concatenate([rho[tuple(selector)][None], flow_wide], 0))

        def pick_rows(start_row):
            return lax.slice_in_dim(slab, start_row, start_row + extent + 1, axis=array_axis)

        fluxes = face_flux(pick_rows(0), pick_rows(1), pick_rows(2), pick_rows(3), normal)
        update = update - (
            lax.slice_in_dim(fluxes, 1, extent + 1, axis=array_axis)
            - lax.slice_in_dim(fluxes, 0, extent, axis=array_axis)
        )

    mean_density = jnp.sum(gathered[:, two_cells]) / total_cells
    step_size = courant / jnp.max(gathered[:, two_cells + 1])
    offset = -coupling * mean_density
    whole = gathered[:, :two_cells].reshape(count_x, count_y, count_z, two_x, two_y, two_z)
    whole = whole.transpose(0, 3, 1, 4, 2, 5).reshape(count_x * two_x, count_y * two_y, count_z * two_z)
    solved = global_level(whole + offset, 16.0)

    one_x, one_y, one_z = own_one.shape
    pick_x = picker(one_x + 8, whole.shape[0], lax.axis_index("gx") * two_x, 2)
    pick_y = picker(one_y + 8, whole.shape[1], lax.axis_index("gy") * two_y, 2)
    pick_z = picker(one_z + 8, whole.shape[2], lax.axis_index("gz") * two_z, 2)
    pick_plane = (pick_x[:, None, :, None] * pick_y[None, :, None, :]).reshape(-1, whole.shape[0] * whole.shape[1])
    correction = jnp.dot(pick_plane, solved.reshape(-1, whole.shape[2]), precision=EXACT)
    correction = lax.dot_general(correction, pick_z, (((1,), (1,)), ((), ())), precision=EXACT)
    correction = correction.reshape(one_x + 8, one_y + 8, one_z + 8)

    wide_one = wide_one + offset
    start_one = jnp.where(parity_of(wide_one.shape, -5) == 0, -4.0 * wide_one / 6.0, 0.0)
    values_one = half_sweep(start_one, inner(wide_one), 4.0, 1, -4) + correction
    values_one = half_sweep(values_one, inner(wide_one, 2), 4.0, 0, -3)
    values_one = half_sweep(values_one, inner(wide_one, 3), 4.0, 1, -2)

    values = inner(swept, 2)
    values = values + jnp.where(parity_of(values.shape, -3) == 0, -offset / 6.0, -offset / 3.0)
    values = values + inner(refine(values_one))
    source = inner(source, 4) + offset
    values = half_sweep(values, source, 1.0, 0, -2)
    values = half_sweep(values, inner(source), 1.0, 1, -1)
    potential_out = inner(values)
    gradients = [
        (values[2:, 1:-1, 1:-1] - values[:-2, 1:-1, 1:-1]) * 0.5,
        (values[1:-1, 2:, 1:-1] - values[1:-1, :-2, 1:-1]) * 0.5,
        (values[1:-1, 1:-1, 2:] - values[1:-1, 1:-1, :-2]) * 0.5,
    ]
    energy_source = -(
        conserved[1] * gradients[0] + conserved[2] * gradients[1] + conserved[3] * gradients[2]
    )
    source_terms = jnp.stack(
        [
            jnp.zeros_like(density),
            -density * gradients[0],
            -density * gradients[1],
            -density * gradients[2],
            energy_source,
        ],
        0,
    )
    updated = conserved + step_size * (update + source_terms)
    return (updated, potential_out)


def solution(mesh):
    in_specs = (P(None, "gx", "gy", "gz"), P("gx", "gy", "gz"))
    out_specs = (P(None, "gx", "gy", "gz"), P("gx", "gy", "gz"))
    return jax.shard_map(shards, mesh=mesh, in_specs=in_specs, out_specs=out_specs, check_vma=False)
```

```python
import functools

import numpy as np
import jax
import jax.numpy as jnp
from jax import lax
from jax.experimental import pallas as pl
from jax.experimental.pallas import tpu as pltpu
from jax.sharding import PartitionSpec as P

LEVELS = 3


gamma_gas = 5.0 / 3.0
courant = 0.4
coupling = 0.01


def primitives(conserved):
    density = conserved[0]
    velocity = conserved[1:4] / density
    kinetic = (
        0.5
        * density
        * (velocity[0] * velocity[0] + velocity[1] * velocity[1] + velocity[2] * velocity[2])
    )
    pressure = (gamma_gas - 1.0) * (conserved[4] - kinetic)
    return jnp.concatenate([density[None], velocity, pressure[None]], 0)


def limited(first, second):
    return 0.5 * (jnp.sign(first) + jnp.sign(second)) * jnp.minimum(jnp.abs(first), jnp.abs(second))


def hllc(left_state, right_state, normal):
    others = ((1, 2), (0, 2), (0, 1))[normal]

    def unpack(primitive):
        density = primitive[0]
        normal_speed = primitive[1 + normal]
        trans_one = primitive[1 + others[0]]
        trans_two = primitive[1 + others[1]]
        pressure = primitive[4]
        energy = pressure / (gamma_gas - 1.0) + 0.5 * density * (
            normal_speed * normal_speed + trans_one * trans_one + trans_two * trans_two
        )
        sound_speed = jnp.sqrt(gamma_gas * pressure / density)
        return (density, normal_speed, trans_one, trans_two, pressure, energy, sound_speed)

    left_terms = unpack(left_state)
    right_terms = unpack(right_state)
    low_wave = jnp.minimum(left_terms[1] - left_terms[6], right_terms[1] - right_terms[6])
    high_wave = jnp.maximum(left_terms[1] + left_terms[6], right_terms[1] + right_terms[6])
    left_mass = left_terms[0] * (low_wave - left_terms[1])
    right_mass = right_terms[0] * (high_wave - right_terms[1])
    star_wave = (
        right_terms[4] - left_terms[4] + left_mass * left_terms[1] - right_mass * right_terms[1]
    ) / (left_mass - right_mass)

    def fluxes(quantities, wave_speed, mass_rate):
        density, normal_speed, trans_one, trans_two, pressure, energy, sound_speed = quantities
        direct = [
            density * normal_speed,
            density * normal_speed * normal_speed + pressure,
            density * normal_speed * trans_one,
            density * normal_speed * trans_two,
            normal_speed * (energy + pressure),
        ]
        stored = [density, density * normal_speed, density * trans_one, density * trans_two, energy]
        factor = mass_rate / (wave_speed - star_wave)
        starred = [
            factor,
            factor * star_wave,
            factor * trans_one,
            factor * trans_two,
            factor
            * (energy / density + (star_wave - normal_speed) * (star_wave + pressure / mass_rate)),
        ]
        return (
            direct,
            [
                direct[member] + wave_speed * (starred[member] - stored[member])
                for member in range(5)
            ],
        )

    left_direct, left_star = fluxes(left_terms, low_wave, left_mass)
    right_direct, right_star = fluxes(right_terms, high_wave, right_mass)
    chosen = [
        jnp.where(
            low_wave >= 0.0,
            left_direct[member],
            jnp.where(
                star_wave >= 0.0,
                left_star[member],
                jnp.where(high_wave > 0.0, right_star[member], right_direct[member]),
            ),
        )
        for member in range(5)
    ]
    momentum = [None, None, None]
    momentum[normal] = chosen[1]
    momentum[others[0]] = chosen[2]
    momentum[others[1]] = chosen[3]
    return jnp.stack([chosen[0]] + momentum + [chosen[4]], 0)


def face_flux(before, centre, after_one, after_two, normal):
    left_state = centre + 0.5 * limited(centre - before, after_one - centre)
    right_state = after_one - 0.5 * limited(after_one - centre, after_two - after_one)
    return hllc(left_state, right_state, normal)

AXES = ("gx", "gy", "gz")
EXACT = lax.Precision.HIGHEST
SIXTH = 1.0 / 6.0
BIG = pltpu.CompilerParams(vmem_limit_bytes=56 * 1024 * 1024)


def shift(payload, axis, step):
    count = lax.axis_size(axis)
    return lax.ppermute(payload, axis, [(i, (i + step) % count) for i in range(count)])


def dot(left, right, dims=((1,), (0,))):
    return lax.dot_general(left, right, (dims, ((), ())), precision=EXACT, preferred_element_type=jnp.float32)


def turn(values, step, axis):
    return pltpu.roll(values, step % values.shape[axis], axis)


def plane_sum(cells):
    total_sum = turn(cells, -1, 0) + turn(cells, 1, 0)
    return total_sum + turn(cells, -1, 1) + turn(cells, 1, 1)


def parity_plane(shape):
    return (lax.broadcasted_iota(jnp.int32, shape, 0) + lax.broadcasted_iota(jnp.int32, shape, 1)) & 1


def slab_sum(ref, place):
    count = ref.shape[0]
    return ref[lax.rem(place + 1, count)] + ref[lax.rem(place + count - 1, count)] + plane_sum(ref[place])


def relax(ref, source_of, spacing_sq, colour, first, count):
    extent = ref.shape[0]
    plane = parity_plane(ref.shape[1:])

    def body(step, carry):
        places = [lax.rem(4 * step + part + (first % extent), extent) for part in range(4)]
        fresh = []
        for place in places:
            renewed = (slab_sum(ref, place) - spacing_sq * source_of(place)) * SIXTH
            fresh.append(jnp.where(plane == ((colour + place) & 1), renewed, ref[place]))
        for place, cells in zip(places, fresh):
            ref[place] = cells
        return carry

    lax.fori_loop(0, (count + 3) // 4, body, 0)


WIDE = 7


def end_columns(extent, width):
    table = np.zeros((16, 128), np.float32)
    table[np.arange(width), np.arange(width)] = 1.0
    table[8 + np.arange(width), extent - width + np.arange(width)] = 1.0
    return table


def place_columns(extent, width):
    table = np.zeros((16, 128), np.float32)
    table[np.arange(width), (extent + np.arange(width)) % 128] = 1.0
    table[8 + np.arange(width), 128 - width + np.arange(width)] = 1.0
    return table


def pack_x_kernel(phi, fluid, head, tail):
    extent = phi.shape[0]
    for start, flow_start, out in ((0, 0, head), (extent - WIDE, extent - 2, tail)):
        out[:WIDE] = phi[start : start + WIDE]
        out[WIDE : 2 * WIDE] = fluid[0, start : start + WIDE]
        for part in range(4):
            out[2 * WIDE + 2 * part : 2 * WIDE + 2 * part + 2] = fluid[1 + part, flow_start : flow_start + 2]


def pack_y_kernel(phi, fluid, flat, left, right, head, tail):
    extent = phi.shape[0]
    lines = extent + 2 * WIDE
    for number, own in ((0, phi), (1, fluid.at[0])):
        base = number * lines
        arrived = pl.ds(number * WIDE, WIDE)
        for rows, out in ((pl.ds(0, 8), head), (pl.ds(8, 8), tail)):
            out[pl.ds(base, extent)] = own[:, rows]
            out[pl.ds(base + extent, WIDE)] = right[arrived, rows]
            out[pl.ds(base + extent + WIDE, WIDE)] = left[arrived, rows]
    for start, out in ((0, head), (14, tail)):
        for part in range(4):
            for row in range(2):
                place = 2 * lines + 2 * (2 * part + row)
                cells = flat.at[1 + part][pl.ds(start + row, extent, stride=16), :]
                out[place : place + 2] = cells.reshape(2, 8, 128)


def pack_z_kernel(phi, fluid, flat, x_left, x_right, y_left, y_right, ends, main, head, tail):
    extent = phi.shape[0]
    lines = extent + 2 * WIDE
    for number, own in ((0, phi), (1, fluid.at[0])):
        base = number * lines
        arrived = pl.ds(number * WIDE, WIDE)
        main[pl.ds(base, extent), :16] = own[...]
        main[pl.ds(base + extent, WIDE), :16] = x_right[arrived]
        main[pl.ds(base + extent + WIDE, WIDE), :16] = x_left[arrived]
        main[pl.ds(base, lines), 16:24] = y_right[pl.ds(base, lines)]
        main[pl.ds(base, lines), 24:] = y_left[pl.ds(base, lines)]
    columns = dot(ends[...], main[...].reshape(2 * lines * 32, 128), ((1,), (1,)))
    head[:, : 64 * lines] = columns[:8]
    tail[:, : 64 * lines] = columns[8:]
    columns = dot(ends[...], flat[1:].reshape(4 * flat.shape[1], 128), ((1,), (1,)))
    head[:, 64 * lines :] = columns[:8]
    tail[:, 64 * lines :] = columns[8:]


def pre_kernel(
    main, z_left, z_right, ends, ends_one, conserved, pair_z, pair_two,
    values, source, one, one_x, one_y, one_head, one_tail, payload,
    sums, halves, swept, rows, *held,
):
    far = (pair_z, pair_two, conserved)
    copies = [pltpu.make_async_copy(ref, near, held[-1].at[number]) for number, (ref, near) in enumerate(zip(far, held))]
    for copy in copies:
        copy.start()
    pair_z, pair_two, conserved = held[:-1]
    lines = main.shape[0] // 2
    extent = lines - 2 * WIDE
    sides = jnp.concatenate([z_right[:, : 64 * lines], z_left[:, : 64 * lines]], 0)
    beside = dot(sides, ends[...], ((0,), (0,))).reshape(2 * lines, 32, 128)
    for number, ref, scale in ((0, values, None), (1, source, coupling)):
        base = number * lines
        gap = extent + WIDE
        ref[gap : 32 - WIDE] = jnp.zeros((32 - WIDE - gap, 32, 256), jnp.float32)
        for cells, columns in ((main, slice(0, 128)), (beside, slice(128, 256))):
            upper = cells[base : base + gap]
            lower = cells[base + gap : base + lines]
            ref[:gap, :, columns] = upper if scale is None else scale * upper
            ref[32 - WIDE :, :, columns] = lower if scale is None else scale * lower

    relax(values, lambda place: source[place], 1.0, 0, -6, extent + 12)
    relax(values, lambda place: source[place], 1.0, 1, -5, extent + 10)

    def defect_pair(step, carry):
        total_sum = jnp.zeros((32, 256), jnp.float32)
        for part in range(2):
            place = 2 * step + part
            total_sum += source[place] - (slab_sum(values, place) - 6.0 * values[place])
        sums[pl.ds(pl.multiple_of(step * 32, 32), 32), :] = total_sum
        return carry

    lax.fori_loop(0, 16, defect_pair, 0)
    for copy in copies:
        copy.wait()
    halves[...] = dot(sums[...], pair_z[...])
    one[...] = (halves[pl.ds(0, 256, stride=2), :] + halves[pl.ds(1, 256, stride=2), :]).reshape(16, 16, 128)
    one_x[...] = one[:8]
    one_y[...] = one[:, :8]
    columns = dot(ends_one[...], one[...].reshape(256, 128), ((1,), (1,)))
    one_head[...] = columns[:8]
    one_tail[...] = columns[8:]

    plane = parity_plane((16, 128))
    for place in range(16):
        swept[place] = jnp.where(plane == (place & 1), one[place] * (-4.0 * SIXTH), 0.0)
    relax(swept, lambda place: one[place], 4.0, 1, 0, 16)
    for step in range(8):
        total_sum = jnp.zeros((16, 128), jnp.float32)
        for part in range(2):
            place = 2 * step + part
            total_sum += one[place] - (slab_sum(swept, place) - 6.0 * swept[place]) * 0.25
        rows[8 * step : 8 * step + 8, :] = total_sum[:8]
    packed = jnp.zeros((8, 128), jnp.float32)
    for part in range(4):
        both = rows[pl.ds(2 * part, 8, stride=8), :] + rows[pl.ds(2 * part + 1, 8, stride=8), :]
        packed += dot(both, pair_two[128 * part : 128 * part + 128, :])

    def measure_slab(place, carry):
        mass, speed = carry
        density = conserved[0, place]
        inverse = 1.0 / density
        first, second, third = conserved[1, place], conserved[2, place], conserved[3, place]
        kinetic = 0.5 * inverse * (first * first + second * second + third * third)
        pressure = (gamma_gas - 1.0) * (conserved[4, place] - kinetic)
        signal = (jnp.abs(first) + jnp.abs(second) + jnp.abs(third)) * inverse
        signal += 3.0 * jnp.sqrt(gamma_gas * pressure * inverse)
        return mass + density, jnp.maximum(speed, signal)

    blank = jnp.zeros((16, 128), jnp.float32)
    mass, speed = lax.fori_loop(0, extent, measure_slab, (blank, blank), unroll=2)
    mass = jnp.sum(jnp.sum(mass, axis=0, keepdims=True), axis=1, keepdims=True)
    speed = jnp.max(jnp.max(speed, axis=0, keepdims=True), axis=1, keepdims=True)
    lane = lax.broadcasted_iota(jnp.int32, (1, 128), 1)
    extra = jnp.where(lane == 0, mass, jnp.where(lane == 1, speed, 0.0))
    count = payload.shape[0] // 5
    for part in range(4):
        payload[pl.ds(part, count, stride=5), :] = jnp.broadcast_to(packed[part : part + 1], (count, 128))
    payload[pl.ds(4, count, stride=5), :] = jnp.broadcast_to(extra, (count, 128))


def cas(extent):
    angle = 2.0 * np.pi / extent * np.outer(np.arange(extent), np.arange(extent))
    return (np.cos(angle) + np.sin(angle)) / np.sqrt(extent)


def eigen(extent, spacing_sq):
    return (2.0 * np.cos(2.0 * np.pi / extent * np.arange(extent)) - 2.0) / spacing_sq


def coarse_tables(planes, groups, spacing_sq):
    half = planes // 2
    line = cas(128)
    same = np.repeat(np.eye(2), 2, 0)
    spread = np.repeat(line, 2, 0).reshape(8, 32, 128)
    forward = np.einsum("ab,gzk->gazbk", same, spread).reshape(1024, 256)
    across = cas(2 * groups).reshape(2 * groups, groups, 2)
    plane = np.einsum("px,qgb->pqbxg", cas(half), across).reshape(2 * groups * half, 2 * groups * half)
    total = (eigen(half, spacing_sq)[:, None] + eigen(2 * groups, spacing_sq)).reshape(-1, 1) + eigen(128, spacing_sq)
    total[0, 0] = 1.0
    inverse = 1.0 / total
    inverse[0, 0] = 0.0
    tables = (0.125 * forward, plane, inverse, plane.T, forward.T)
    return tuple(np.ascontiguousarray(table, dtype=np.float32) for table in tables)


def pick_table():
    table = np.zeros((3, 4, 32, 4, 128), np.float32)
    for line in range(4):
        for cell in range(32):
            table[0, line, cell, line, 2 * cell : 2 * cell + 2] = 1.0
        for cell in range(2):
            table[1, line, cell, line, 64 + 2 * cell : 66 + 2 * cell] = 1.0
            table[2, line, 30 + cell, line, 124 + 2 * cell : 126 + 2 * cell] = 1.0
    return table.reshape(384, 512)


def post_kernel(
    planes, groups, cells_total,
    where_ref, gathered, values, source, one_own, x_left, x_right, y_left, y_right, z_left, z_right, conserved, update,
    to_line, to_plane, inverse, from_plane, from_line, pick, place_one, refine_z,
    updated, potential_out,
    coarse, rhs, stage, chosen, extra, one_rhs, one, fine_low, fine_high, work,
    *held,
):
    far = (to_line, to_plane, inverse, from_plane, from_line, pick, one_own, x_left, x_right, y_left, y_right, z_left, z_right)
    far += (place_one, refine_z, values, source, conserved, update)
    arrivals = held[-1]
    copies = [pltpu.make_async_copy(ref, near, arrivals.at[number]) for number, (ref, near) in enumerate(zip(far, held))]
    for copy in copies:
        copy.start()
    to_line, to_plane, inverse, from_plane, from_line, pick, one_own, x_left, x_right, y_left, y_right, z_left, z_right = held[:13]
    place_one, refine_z, values, source, conserved, update = held[13:-1]

    last = gathered[pl.ds(4, gathered.shape[0] // 5, stride=5), :]
    lane_row = lax.broadcasted_iota(jnp.int32, (1, 128), 1)
    mass = jnp.sum(jnp.where(lane_row == 0, jnp.sum(last, axis=0, keepdims=True), 0.0), axis=1, keepdims=True)
    speed = jnp.sum(jnp.where(lane_row == 1, jnp.max(last, axis=0, keepdims=True), 0.0), axis=1, keepdims=True)
    offset = mass * (-coupling / cells_total)
    step_size = courant / speed

    spacing_sq = 16.0
    lane = lax.broadcasted_iota(jnp.int32, (8, 128), 1)
    cell = lane & 31
    plane = (cell + (lane >> 5)) & 1

    def tile(place, group):
        return pl.ds(pl.multiple_of((place * groups + group) * 8, 8), 8)

    def tile_sum(place, group):
        centre = coarse[tile(place, group), :]
        total_sum = coarse[tile(lax.rem(place + 1, planes), group), :]
        total_sum += coarse[tile(lax.rem(place + planes - 1, planes), group), :]
        after = coarse[tile(place, (group + 1) % groups), :]
        before = coarse[tile(place, (group + groups - 1) % groups), :]
        total_sum += turn(jnp.where(lane < 32, after, centre), -32, 1)
        total_sum += turn(jnp.where(lane >= 96, before, centre), 32, 1)
        total_sum += jnp.where(cell == 31, turn(turn(centre, -1, 0), 31, 1), turn(centre, -1, 1))
        total_sum += jnp.where(cell == 0, turn(turn(centre, 1, 0), -31, 1), turn(centre, 1, 1))
        return centre, total_sum

    def coarse_relax(colour):
        def body(place, carry):
            wanted = plane == ((colour + place) & 1)
            fresh = []
            for group in range(groups):
                centre, total_sum = tile_sum(place, group)
                renewed = (total_sum - spacing_sq * rhs[tile(place, group), :]) * SIXTH
                fresh.append(jnp.where(wanted, renewed, centre))
            for group in range(groups):
                coarse[tile(place, group), :] = fresh[group]
            return carry

        lax.fori_loop(0, planes, body, 0)

    for place in range(planes):
        for group in range(groups):
            first_row = ((place // 4) * groups + group) * 8
            cells = gathered[pl.ds(5 * first_row + place % 4, 8, stride=5), :] + offset
            here = pl.ds((place * groups + group) * 8, 8)
            rhs[here, :] = cells
            coarse[here, :] = jnp.where(plane == (place & 1), cells * (-spacing_sq * SIXTH), 0.0)
    coarse_relax(1)

    def defect_pair(step, carry):
        for group in range(groups):
            total = jnp.zeros((8, 128), jnp.float32)
            for part in range(2):
                place = 2 * step + part
                centre, total_sum = tile_sum(place, group)
                total += rhs[tile(place, group), :] - (total_sum - 6.0 * centre) * (1.0 / spacing_sq)
            stage[tile(step, group), :] = total
        return carry

    half = planes // 2
    lines = half * groups
    for copy in copies[:5]:
        copy.wait()
    lax.fori_loop(0, half, defect_pair, 0)
    modes = jnp.zeros((lines, 256), jnp.float32)
    for part in range(8):
        modes += dot(stage[pl.ds(part, lines, stride=8), :], to_line[128 * part : 128 * part + 128, :])
    modes = jnp.concatenate([modes[:, :128], modes[:, 128:]], 0)
    modes = dot(from_plane[...], dot(to_plane[...], modes) * inverse[...])
    modes = jnp.concatenate([modes[:lines], modes[lines:]], 1)
    for part in range(8):
        stage[pl.ds(part, lines, stride=8), :] = dot(modes, from_line[:, 128 * part : 128 * part + 128])

    def add_back(step, carry):
        for group in range(groups):
            correction = stage[tile(step, group), :]
            for part in range(2):
                coarse[tile(2 * step + part, group), :] += correction
        return carry

    lax.fori_loop(0, half, add_back, 0)
    coarse_relax(0)
    coarse_relax(1)

    my_x, my_y, my_z = where_ref[0], where_ref[1], where_ref[2]
    for number, along_y in enumerate((0, 1, groups - 1)):
        for row, along_x in enumerate((0, 1, 2, 3, 4, 5, planes - 2, planes - 1)):
            for column, along_z in enumerate((0, 1, 7)):
                place = lax.rem(4 * my_x + along_x, planes)
                group = lax.rem(my_y + along_y, groups)
                line = lax.rem(my_z + along_z, 8)
                chosen[8 * number + row : 8 * number + row + 1, 128 * column : 128 * column + 128] = coarse[
                    pl.ds((place * groups + group) * 8 + line, 1), :
                ]
    for copy in copies[5:15]:
        copy.wait()
    picked = dot(chosen[...], pick[...])
    for number, line, slot in ((0, 0, 0), (0, 1, 2), (0, 2, 4), (0, 3, 6), (1, 0, 8), (1, 1, 10), (2, 2, 20), (2, 3, 22)):
        rows = picked[8 * number : 8 * number + 8, 128 * line : 128 * line + 128]
        for part in range(2):
            for twice in range(2):
                extra[pl.ds(24 * part + slot + twice, 8, stride=48), :] = rows

    sides = jnp.concatenate([z_right[...], z_left[...]], 0)
    beside = dot(sides, place_one[...], ((0,), (0,))).reshape(16, 16, 128)
    line_one = lax.broadcasted_iota(jnp.int32, (24, 128), 0)
    lane_one = lax.broadcasted_iota(jnp.int32, (24, 128), 1)
    plane_one = (line_one + lane_one) & 1
    from_z = jnp.logical_and(lane_one >= 64, jnp.logical_or(line_one < 10, line_one >= 22))
    for place in range(24):
        if place < 10 or place >= 22:
            row = place if place < 10 else place - 8
            cells = jnp.concatenate([one_own[row, :8], y_right[row], y_left[row]], 0)
            sideways = beside[row]
            cells = jnp.where(from_z, jnp.concatenate([sideways, sideways[8:]], 0), cells)
        elif place < 13 or place >= 19:
            cells = x_right[place - 8] if place < 13 else x_left[place - 16]
            cells = jnp.concatenate([cells, cells[8:]], 0)
        else:
            cells = jnp.zeros((24, 128), jnp.float32)
        cells = cells + offset
        one_rhs[place] = cells
        one[place] = jnp.where(plane_one == (place & 1), cells * (-4.0 * SIXTH), 0.0)
    relax(one, lambda place: one_rhs[place], 4.0, 1, -4, 16)
    for row in range(16):
        place = row if row < 12 else row + 8
        one[place] += extra[24 * row : 24 * row + 24, :]
    relax(one, lambda place: one_rhs[place], 4.0, 0, -3, 14)
    relax(one, lambda place: one_rhs[place], 4.0, 1, -2, 12)

    wide = jnp.concatenate([one[0:10], one[22:24]], 0).reshape(288, 128)
    wide = dot(wide, refine_z[...])
    for row in range(12):
        for part, fine in ((0, fine_low), (1, fine_high)):
            cells = wide[24 * row : 24 * row + 24, 128 * part : 128 * part + 128]
            for twice in range(2):
                fine[pl.ds(32 * row + twice, 8, stride=2), :] = cells[:8]
                fine[pl.ds(32 * row + 16 + twice, 4, stride=2), :] = cells[8:12]
                fine[pl.ds(32 * row + 24 + twice, 4, stride=2), :] = cells[20:24]
    plane_fine = parity_plane((32, 256))
    for copy in copies[15:]:
        copy.wait()
    for place in tuple(range(20)) + tuple(range(28, 32)):
        row = place // 2 if place < 20 else place // 2 - 4
        lift = jnp.concatenate([fine_low[32 * row : 32 * row + 32, :], fine_high[32 * row : 32 * row + 32, :]], 1)
        moved = jnp.where(plane_fine == (place & 1), offset * (-SIXTH), offset * (-2.0 * SIXTH))
        work[place] = values[place] + (lift + moved)
    extent = potential_out.shape[0]
    relax(work, lambda place: source[place] + offset, 1.0, 0, -2, extent + 4)
    relax(work, lambda place: source[place] + offset, 1.0, 1, -1, extent + 2)

    def finish(place, carry):
        cells = work[place]
        after, before = work[lax.rem(place + 1, 32)], work[lax.rem(place + 31, 32)]
        along_x = (after[:16, :128] - before[:16, :128]) * 0.5
        along_y = ((turn(cells, -1, 0) - turn(cells, 1, 0)) * 0.5)[:16, :128]
        along_z = ((turn(cells, -1, 1) - turn(cells, 1, 1)) * 0.5)[:16, :128]
        potential_out[place] = cells[:16, :128]
        density = conserved[0, place]
        first, second, third = conserved[1, place], conserved[2, place], conserved[3, place]
        energy_source = first * along_x + second * along_y + third * along_z
        updated[0, place] = density + step_size * update[0, place]
        updated[1, place] = first + step_size * (update[1, place] - density * along_x)
        updated[2, place] = second + step_size * (update[2, place] - density * along_y)
        updated[3, place] = third + step_size * (update[3, place] - density * along_z)
        updated[4, place] = conserved[4, place] + step_size * (update[4, place] - energy_source)
        return carry

    lax.fori_loop(0, extent, finish, 0, unroll=2)


def widen(cells, left, right):
    width = left.shape[0]
    flat = dot(jnp.concatenate([left, right], 0), np.eye(2 * width, dtype=np.float32), ((0,), (0,)))
    flat = flat.reshape(cells.shape[:-1] + (2 * width,))
    return jnp.concatenate([flat[..., :width], cells, flat[..., width:]], -1)


def call(kernel, shapes, scratch=(), operands=None, late=()):
    extra = {}
    if late:
        specs = [pl.BlockSpec(memory_space=pl.ANY if number in late else pltpu.VMEM) for number in range(max(late) + 1)]
        extra = dict(in_specs=specs)
    if operands is not None:
        specs = [pl.BlockSpec(shape, functools.partial(lambda rank, step: (0,) * rank, len(shape))) for shape in operands]
        results = [pl.BlockSpec(shape, functools.partial(lambda rank, step: (0,) * rank, len(shape))) for shape in shapes]
        extra = dict(grid=(1,), in_specs=specs, out_specs=results)
    return pl.pallas_call(
        kernel,
        **extra,
        out_shape=[jax.ShapeDtypeStruct(shape, jnp.float32) for shape in shapes],
        scratch_shapes=[pltpu.VMEM(shape, jnp.float32) for shape in scratch]
        + ([pltpu.SemaphoreType.DMA((len(late),))] if late else []),
        compiler_params=BIG,
    )


def halved(fine):
    return np.repeat(np.eye(fine // 2, dtype=np.float32), 2, 0)


def shards(conserved, potential):
    cells_x, cells_y, cells_z = potential.shape
    count_x, count_y, count_z = (lax.axis_size(axis) for axis in AXES)
    devices = count_x * count_y * count_z
    lines = cells_x + 2 * WIDE
    block, whole, flat = (cells_x, cells_y, cells_z), conserved.shape, (5, cells_x * cells_y, cells_z)
    side, slab, ends = (2 * WIDE + 8, cells_y, cells_z), (2 * lines + 16, 8, cells_z), end_columns(cells_z, WIDE)
    fluid_rows = conserved.reshape(flat)

    head, tail = call(pack_x_kernel, [side] * 2, (), [block, whole])(potential, conserved)
    x_left, x_right = shift(tail, "gx", 1), shift(head, "gx", -1)
    head, tail = call(pack_y_kernel, [slab] * 2, (), [block, (1,) + block, flat, side, side])(
        potential, conserved, fluid_rows, x_left, x_right
    )
    y_left, y_right = shift(tail, "gy", 1), shift(head, "gy", -1)
    columns = (8, 64 * lines + 4 * cells_x * cells_y)
    main, head, tail = call(
        pack_z_kernel,
        [(2 * lines, 32, cells_z), columns, columns],
        (),
        [block, (1,) + block, flat, side, side, slab, slab, ends.shape],
    )(potential, conserved, fluid_rows, x_left, x_right, y_left, y_right, ends)
    z_left, z_right = shift(tail, "gz", 1), shift(head, "gz", -1)

    pair_two = np.zeros((4, 128, 4, 32), np.float32)
    for part in range(4):
        pair_two[part, :64, part] = 0.125 * halved(64)
    window = (32, 32, 2 * cells_z)
    sizes = [window, window, (16, 16, 128), (8, 16, 128), (16, 8, 128), (8, 256), (8, 256), (devices * 5, 128)]
    tables = (0.125 * halved(256), pair_two.reshape(512, 128))
    values, source, one, one_x, one_y, one_head, one_tail, payload = call(
        pre_kernel,
        sizes,
        [(512, 256), (512, 128), (16, 16, 128), (64, 128), tables[0].shape, tables[1].shape, whole],
        late=(5, 6, 7),
    )(main, z_left, z_right, ends, end_columns(64, 5), conserved, *tables)

    one_halo = [shift(one_x, "gx", 1), shift(one_x, "gx", -1), shift(one_y, "gy", 1), shift(one_y, "gy", -1)]
    one_halo += [shift(one_tail, "gz", 1), shift(one_head, "gz", -1)]
    gathered = lax.all_to_all(payload.reshape(devices, 1, 640), AXES, 0, 0, tiled=True).reshape(devices * 5, 128)

    one_halo, fluid, main, *sides = lax.optimization_barrier(
        (one_halo, conserved, main, x_left, x_right, y_left, y_right, z_left, z_right)
    )
    rho = main[lines:]

    def along_x(arrived):
        return arrived[2 * WIDE :].reshape(4, 2, cells_y, cells_z)

    def along_y(arrived):
        return arrived[2 * lines :].reshape(4, 2, cells_x, cells_z).swapaxes(1, 2)

    def along_z(arrived, start):
        used = arrived[start : start + 2]
        thin = used[:, 32 * lines : 32 * (lines + cells_x)].reshape(2, cells_x, 32)[:, :, :16].reshape(2, -1)
        return jnp.concatenate([thin, used[:, 64 * lines :]], 1)

    flow = fluid[1:]
    wide_x = jnp.concatenate([rho[-2:, :16], rho[: cells_x + 2, :16]], 0)[None]
    wide_x = jnp.concatenate([wide_x, jnp.concatenate([along_x(sides[0]), flow, along_x(sides[1])], 1)], 0)
    wide_y = jnp.concatenate([rho[:cells_x, 30:], rho[:cells_x, :18]], 1)[None]
    wide_y = jnp.concatenate([wide_y, jnp.concatenate([along_y(sides[2]), flow, along_y(sides[3])], 2)], 0)
    wide_z = widen(fluid, along_z(sides[4], WIDE - 2), along_z(sides[5], 0))
    update = jnp.zeros_like(conserved)
    for normal, wide in enumerate((wide_x, wide_y, wide_z)):
        array_axis = 1 + normal
        extent = conserved.shape[array_axis]
        slab = primitives(wide)

        def pick_rows(start_row):
            return lax.slice_in_dim(slab, start_row, start_row + extent + 1, axis=array_axis)

        fluxes = face_flux(pick_rows(0), pick_rows(1), pick_rows(2), pick_rows(3), normal)
        update = update - (
            lax.slice_in_dim(fluxes, 1, extent + 1, axis=array_axis)
            - lax.slice_in_dim(fluxes, 0, extent, axis=array_axis)
        )

    planes, groups = 4 * count_x, count_y
    position = jnp.stack([lax.axis_index(axis) for axis in AXES]).astype(jnp.int32)
    operands = (gathered, values, source, one, *one_halo, conserved, update)
    operands += coarse_tables(planes, groups, 64.0) + (pick_table(), place_columns(64, 5), halved(256).T)
    order = (12, 13, 14, 15, 16, 17, 3, 4, 5, 6, 7, 8, 9, 18, 19, 1, 2, 10, 11)
    tiles = planes * groups * 8
    updated, potential_out = pl.pallas_call(
        functools.partial(post_kernel, planes, groups, float(devices * cells_x * cells_y * cells_z)),
        out_shape=[jax.ShapeDtypeStruct(array.shape, jnp.float32) for array in (conserved, potential)],
        in_specs=[pl.BlockSpec(memory_space=pltpu.SMEM)]
        + [pl.BlockSpec(memory_space=pl.ANY if number else pltpu.VMEM) for number in range(len(operands))],
        scratch_shapes=[
            pltpu.VMEM(shape, jnp.float32)
            for shape in (
                (tiles, 128), (tiles, 128), (tiles // 2, 128), (24, 384), (384, 128),
                (24, 24, 128), (24, 24, 128), (384, 128), (384, 128), (32, 32, 256),
            )
        ]
        + [pltpu.VMEM(operands[number].shape, jnp.float32) for number in order]
        + [pltpu.SemaphoreType.DMA((len(order),))],
        compiler_params=BIG,
    )(position, *operands)
    return (updated, potential_out)


def solution(mesh):
    in_specs = (P(None, "gx", "gy", "gz"), P("gx", "gy", "gz"))
    out_specs = (P(None, "gx", "gy", "gz"), P("gx", "gy", "gz"))
    return jax.shard_map(shards, mesh=mesh, in_specs=in_specs, out_specs=out_specs, check_vma=False)
```

```python
import functools

import numpy as np
import jax
import jax.numpy as jnp
from jax import lax
from jax.experimental import pallas as pl
from jax.experimental.pallas import tpu as pltpu
from jax.sharding import PartitionSpec as P

LEVELS = 3


gamma_gas = 5.0 / 3.0
courant = 0.4
coupling = 0.01


def primitives(density, first, second, third, energy):
    inverse = 1.0 / density
    kinetic = 0.5 * inverse * (first * first + second * second + third * third)
    pressure = (gamma_gas - 1.0) * (energy - kinetic)
    return [density, first * inverse, second * inverse, third * inverse, pressure]


def limited(first, second):
    return jnp.maximum(0.0, jnp.minimum(first, second)) + jnp.minimum(0.0, jnp.maximum(first, second))


def face_flux(before, centre, after_one, after_two, normal):
    lefts, rights = [], []
    for one, two, three, four in zip(before, centre, after_one, after_two):
        middle = three - two
        lefts.append(two + 0.5 * limited(two - one, middle))
        rights.append(three - 0.5 * limited(middle, four - three))
    along = 1 + normal
    others = [member for member in (1, 2, 3) if member != along]

    def unpack(state):
        density, speed, pressure = state[0], state[along], state[4]
        inverse = 1.0 / density
        squares = speed * speed + state[others[0]] * state[others[0]] + state[others[1]] * state[others[1]]
        energy = pressure * (1.0 / (gamma_gas - 1.0)) + 0.5 * density * squares
        return inverse, energy, jnp.sqrt(gamma_gas * pressure * inverse)

    left_inverse, left_energy, left_sound = unpack(lefts)
    right_inverse, right_energy, right_sound = unpack(rights)
    left_speed, right_speed = lefts[along], rights[along]
    low_wave = jnp.minimum(left_speed - left_sound, right_speed - right_sound)
    high_wave = jnp.maximum(left_speed + left_sound, right_speed + right_sound)
    left_mass = lefts[0] * (low_wave - left_speed)
    right_mass = rights[0] * (high_wave - right_speed)
    star_wave = (rights[4] - lefts[4] + left_mass * left_speed - right_mass * right_speed) / (left_mass - right_mass)
    from_left = jnp.logical_or(low_wave >= 0.0, star_wave >= 0.0)
    state = [jnp.where(from_left, one, two) for one, two in zip(lefts, rights)]
    inverse = jnp.where(from_left, left_inverse, right_inverse)
    energy = jnp.where(from_left, left_energy, right_energy)
    wave = jnp.where(from_left, low_wave, high_wave)
    rate = jnp.where(from_left, left_mass, right_mass)
    unstarred = jnp.where(from_left, -low_wave, high_wave) <= 0.0
    density, speed, pressure = state[0], state[along], state[4]
    carried = density * speed
    spread = 1.0 / (wave - star_wave)
    factor = rate * spread
    starred_energy = factor * (energy * inverse) + (star_wave - speed) * (factor * star_wave + pressure * spread)

    def jump(starred, stored):
        return jnp.where(unstarred, 0.0, wave * (starred - stored))

    mass_flux = carried + jump(factor, density)
    flux = [None] * 5
    flux[0] = mass_flux
    flux[along] = carried * speed + pressure + jump(factor * star_wave, carried)
    for member in others:
        flux[member] = state[member] * mass_flux
    flux[4] = speed * (energy + pressure) + jump(starred_energy, energy)
    return flux


AXES = ("gx", "gy", "gz")
EXACT = lax.Precision.HIGHEST
SIXTH = 1.0 / 6.0
SMALL = pltpu.CompilerParams(vmem_limit_bytes=20 * 1024 * 1024)
BIG = pltpu.CompilerParams(vmem_limit_bytes=56 * 1024 * 1024)


def shift(payload, axis, step):
    count = lax.axis_size(axis)
    return lax.ppermute(payload, axis, [(i, (i + step) % count) for i in range(count)])


def dot(left, right, dims=((1,), (0,))):
    return lax.dot_general(left, right, (dims, ((), ())), precision=EXACT, preferred_element_type=jnp.float32)


def turn(values, step, axis):
    return pltpu.roll(values, step % values.shape[axis], axis)


def plane_sum(cells):
    total_sum = turn(cells, -1, 0) + turn(cells, 1, 0)
    return total_sum + turn(cells, -1, 1) + turn(cells, 1, 1)


def parity_plane(shape):
    return (lax.broadcasted_iota(jnp.int32, shape, 0) + lax.broadcasted_iota(jnp.int32, shape, 1)) & 1


def slab_sum(ref, place):
    count = ref.shape[0]
    return ref[lax.rem(place + 1, count)] + ref[lax.rem(place + count - 1, count)] + plane_sum(ref[place])


def relax(ref, source_of, spacing_sq, colour, first, count):
    extent = ref.shape[0]
    plane = parity_plane(ref.shape[1:])

    def body(step, carry):
        places = [lax.rem(4 * step + part + (first % extent), extent) for part in range(4)]
        fresh = []
        for place in places:
            renewed = (slab_sum(ref, place) - spacing_sq * source_of(place)) * SIXTH
            fresh.append(jnp.where(plane == ((colour + place) & 1), renewed, ref[place]))
        for place, cells in zip(places, fresh):
            ref[place] = cells
        return carry

    lax.fori_loop(0, (count + 3) // 4, body, 0)


WIDE = 7


def end_columns(extent, width):
    table = np.zeros((16, 128), np.float32)
    table[np.arange(width), np.arange(width)] = 1.0
    table[8 + np.arange(width), extent - width + np.arange(width)] = 1.0
    return table


def place_columns(extent, width):
    table = np.zeros((16, 128), np.float32)
    table[np.arange(width), (extent + np.arange(width)) % 128] = 1.0
    table[8 + np.arange(width), 128 - width + np.arange(width)] = 1.0
    return table


def pack_x_kernel(phi, fluid, head, tail):
    extent = phi.shape[0]
    for start, flow_start, out in ((0, 0, head), (extent - WIDE, extent - 2, tail)):
        out[:WIDE] = phi[start : start + WIDE]
        out[WIDE : 2 * WIDE] = fluid[0, start : start + WIDE]
        for part in range(4):
            out[2 * WIDE + 2 * part : 2 * WIDE + 2 * part + 2] = fluid[1 + part, flow_start : flow_start + 2]


def pack_y_kernel(phi, fluid, flat, left, right, head, tail):
    extent = phi.shape[0]
    lines = extent + 2 * WIDE
    for number, own in ((0, phi), (1, fluid.at[0])):
        base = number * lines
        arrived = pl.ds(number * WIDE, WIDE)
        for rows, out in ((pl.ds(0, 8), head), (pl.ds(8, 8), tail)):
            out[pl.ds(base, extent)] = own[:, rows]
            out[pl.ds(base + extent, WIDE)] = right[arrived, rows]
            out[pl.ds(base + extent + WIDE, WIDE)] = left[arrived, rows]
    for start, out in ((0, head), (14, tail)):
        for part in range(4):
            for row in range(2):
                place = 2 * lines + 2 * (2 * part + row)
                cells = flat.at[1 + part][pl.ds(start + row, extent, stride=16), :]
                out[place : place + 2] = cells.reshape(2, 8, 128)


def pack_z_kernel(phi, fluid, flat, x_left, x_right, y_left, y_right, ends, main, head, tail):
    extent = phi.shape[0]
    lines = extent + 2 * WIDE
    for number, own in ((0, phi), (1, fluid.at[0])):
        base = number * lines
        arrived = pl.ds(number * WIDE, WIDE)
        main[pl.ds(base, extent), :16] = own[...]
        main[pl.ds(base + extent, WIDE), :16] = x_right[arrived]
        main[pl.ds(base + extent + WIDE, WIDE), :16] = x_left[arrived]
        main[pl.ds(base, lines), 16:24] = y_right[pl.ds(base, lines)]
        main[pl.ds(base, lines), 24:] = y_left[pl.ds(base, lines)]
    columns = dot(ends[...], main[...].reshape(2 * lines * 32, 128), ((1,), (1,)))
    head[:, : 64 * lines] = columns[:8]
    tail[:, : 64 * lines] = columns[8:]
    columns = dot(ends[...], flat[1:].reshape(4 * flat.shape[1], 128), ((1,), (1,)))
    head[:, 64 * lines :] = columns[:8]
    tail[:, 64 * lines :] = columns[8:]


def pre_kernel(
    main, z_left, z_right, ends, ends_one, conserved, pair_z, pair_two,
    values_out, source_out, one, one_x, one_y, one_head, one_tail, payload,
    values, source, sums, halves, swept, rows, leaving,
):
    lines = main.shape[0] // 2
    extent = lines - 2 * WIDE
    sides = jnp.concatenate([z_right[:, : 64 * lines], z_left[:, : 64 * lines]], 0)
    beside = dot(sides, ends[...], ((0,), (0,))).reshape(2 * lines, 32, 128)
    for number, ref, scale in ((0, values, None), (1, source, coupling)):
        base = number * lines
        gap = extent + WIDE
        ref[gap : 32 - WIDE] = jnp.zeros((32 - WIDE - gap, 32, 256), jnp.float32)
        for cells, columns in ((main, slice(0, 128)), (beside, slice(128, 256))):
            upper = cells[base : base + gap]
            lower = cells[base + gap : base + lines]
            ref[:gap, :, columns] = upper if scale is None else scale * upper
            ref[32 - WIDE :, :, columns] = lower if scale is None else scale * lower

    source_copy = pltpu.make_async_copy(source, source_out, leaving.at[0])
    source_copy.start()
    relax(values, lambda place: source[place], 1.0, 0, -6, extent + 12)
    relax(values, lambda place: source[place], 1.0, 1, -5, extent + 10)
    values_copy = pltpu.make_async_copy(values, values_out, leaving.at[1])
    values_copy.start()

    sums[10 * 32 : 14 * 32, :] = jnp.zeros((4 * 32, 256), jnp.float32)

    def defect_pair(turned, carry):
        step = lax.rem(turned + 14, 16)
        total_sum = jnp.zeros((32, 256), jnp.float32)
        for part in range(2):
            place = 2 * step + part
            total_sum += source[place] - (slab_sum(values, place) - 6.0 * values[place])
        sums[pl.ds(pl.multiple_of(step * 32, 32), 32), :] = total_sum
        return carry

    lax.fori_loop(0, 12, defect_pair, 0, unroll=2)
    halves[...] = dot(sums[...], pair_z[...])
    one[...] = (halves[pl.ds(0, 256, stride=2), :] + halves[pl.ds(1, 256, stride=2), :]).reshape(16, 16, 128)
    one_x[...] = one[:8]
    one_y[...] = one[:, :8]
    columns = dot(ends_one[...], one[...].reshape(256, 128), ((1,), (1,)))
    one_head[...] = columns[:8]
    one_tail[...] = columns[8:]

    plane = parity_plane((16, 128))
    for place in range(16):
        swept[place] = jnp.where(plane == (place & 1), one[place] * (-4.0 * SIXTH), 0.0)
    relax(swept, lambda place: one[place], 4.0, 1, 0, 16)
    for step in range(8):
        total_sum = jnp.zeros((16, 128), jnp.float32)
        for part in range(2):
            place = 2 * step + part
            total_sum += one[place] - (slab_sum(swept, place) - 6.0 * swept[place]) * 0.25
        rows[8 * step : 8 * step + 8, :] = total_sum[:8]
    packed = jnp.zeros((8, 128), jnp.float32)
    for part in range(4):
        both = rows[pl.ds(2 * part, 8, stride=8), :] + rows[pl.ds(2 * part + 1, 8, stride=8), :]
        packed += dot(both, pair_two[128 * part : 128 * part + 128, :])

    def measure_slab(place, carry):
        mass, speed = carry
        density = conserved[0, place]
        inverse = 1.0 / density
        first, second, third = conserved[1, place], conserved[2, place], conserved[3, place]
        kinetic = 0.5 * inverse * (first * first + second * second + third * third)
        pressure = (gamma_gas - 1.0) * (conserved[4, place] - kinetic)
        signal = (jnp.abs(first) + jnp.abs(second) + jnp.abs(third)) * inverse
        signal += 3.0 * jnp.sqrt(gamma_gas * pressure * inverse)
        return mass + density, jnp.maximum(speed, signal)

    blank = jnp.zeros((16, 128), jnp.float32)
    mass, speed = lax.fori_loop(0, extent, measure_slab, (blank, blank), unroll=2)
    mass = jnp.sum(jnp.sum(mass, axis=0, keepdims=True), axis=1, keepdims=True)
    speed = jnp.max(jnp.max(speed, axis=0, keepdims=True), axis=1, keepdims=True)
    lane = lax.broadcasted_iota(jnp.int32, (1, 128), 1)
    extra = jnp.where(lane == 0, mass, jnp.where(lane == 1, speed, 0.0))
    count = payload.shape[0] // 5
    for part in range(4):
        payload[pl.ds(part, count, stride=5), :] = jnp.broadcast_to(packed[part : part + 1], (count, 128))
    payload[pl.ds(4, count, stride=5), :] = jnp.broadcast_to(extra, (count, 128))
    source_copy.wait()
    values_copy.wait()


def cas(extent):
    angle = 2.0 * np.pi / extent * np.outer(np.arange(extent), np.arange(extent))
    return (np.cos(angle) + np.sin(angle)) / np.sqrt(extent)


def eigen(extent, spacing_sq):
    return (2.0 * np.cos(2.0 * np.pi / extent * np.arange(extent)) - 2.0) / spacing_sq


def coarse_tables(planes, groups, spacing_sq):
    half = planes // 2
    line = cas(128)
    same = np.repeat(np.eye(2), 2, 0)
    spread = np.repeat(line, 2, 0).reshape(8, 32, 128)
    forward = np.einsum("ab,gzk->gazbk", same, spread).reshape(1024, 256)
    across = cas(2 * groups).reshape(2 * groups, groups, 2)
    plane = np.einsum("px,qgb->pqbxg", cas(half), across).reshape(2 * groups * half, 2 * groups * half)
    total = (eigen(half, spacing_sq)[:, None] + eigen(2 * groups, spacing_sq)).reshape(-1, 1) + eigen(128, spacing_sq)
    total[0, 0] = 1.0
    inverse = 1.0 / total
    inverse[0, 0] = 0.0
    tables = (0.125 * forward, plane, inverse, plane.T, forward.T)
    return tuple(np.ascontiguousarray(table, dtype=np.float32) for table in tables)


def pick_table():
    table = np.zeros((3, 4, 32, 4, 128), np.float32)
    for line in range(4):
        for cell in range(32):
            table[0, line, cell, line, 2 * cell : 2 * cell + 2] = 1.0
        for cell in range(2):
            table[1, line, cell, line, 64 + 2 * cell : 66 + 2 * cell] = 1.0
            table[2, line, 30 + cell, line, 124 + 2 * cell : 126 + 2 * cell] = 1.0
    return table.reshape(384, 512)


def post_kernel(
    planes, groups, cells_total,
    where_ref, gathered, values, source, one_own, x_left, x_right, y_left, y_right, z_left, z_right, conserved, update,
    to_line, to_plane, inverse, from_plane, from_line, pick, place_one, refine_z,
    updated, potential_out,
    coarse, rhs, stage, chosen, extra, one_rhs, one, fine_low, fine_high, work,
    *held,
):
    far = (to_line, to_plane, inverse, from_plane, from_line, pick, one_own, x_left, x_right, y_left, y_right, z_left, z_right)
    far += (place_one, refine_z, values, source, conserved, update)
    arrivals = held[-1]
    copies = [pltpu.make_async_copy(ref, near, arrivals.at[number]) for number, (ref, near) in enumerate(zip(far, held))]
    for copy in copies:
        copy.start()
    to_line, to_plane, inverse, from_plane, from_line, pick, one_own, x_left, x_right, y_left, y_right, z_left, z_right = held[:13]
    place_one, refine_z, values, source, conserved, update = held[13:-1]

    last = gathered[pl.ds(4, gathered.shape[0] // 5, stride=5), :]
    lane_row = lax.broadcasted_iota(jnp.int32, (1, 128), 1)
    mass = jnp.sum(jnp.where(lane_row == 0, jnp.sum(last, axis=0, keepdims=True), 0.0), axis=1, keepdims=True)
    speed = jnp.sum(jnp.where(lane_row == 1, jnp.max(last, axis=0, keepdims=True), 0.0), axis=1, keepdims=True)
    offset = mass * (-coupling / cells_total)
    step_size = courant / speed

    spacing_sq = 16.0
    lane = lax.broadcasted_iota(jnp.int32, (8, 128), 1)
    cell = lane & 31
    plane = (cell + (lane >> 5)) & 1

    def tile(place, group):
        return pl.ds(pl.multiple_of((place * groups + group) * 8, 8), 8)

    def tile_sum(place, group):
        centre = coarse[tile(place, group), :]
        total_sum = coarse[tile(lax.rem(place + 1, planes), group), :]
        total_sum += coarse[tile(lax.rem(place + planes - 1, planes), group), :]
        after = coarse[tile(place, (group + 1) % groups), :]
        before = coarse[tile(place, (group + groups - 1) % groups), :]
        total_sum += turn(jnp.where(lane < 32, after, centre), -32, 1)
        total_sum += turn(jnp.where(lane >= 96, before, centre), 32, 1)
        total_sum += jnp.where(cell == 31, turn(turn(centre, -1, 0), 31, 1), turn(centre, -1, 1))
        total_sum += jnp.where(cell == 0, turn(turn(centre, 1, 0), -31, 1), turn(centre, 1, 1))
        return centre, total_sum

    def coarse_relax(colour):
        def body(place, carry):
            wanted = plane == ((colour + place) & 1)
            fresh = []
            for group in range(groups):
                centre, total_sum = tile_sum(place, group)
                renewed = (total_sum - spacing_sq * rhs[tile(place, group), :]) * SIXTH
                fresh.append(jnp.where(wanted, renewed, centre))
            for group in range(groups):
                coarse[tile(place, group), :] = fresh[group]
            return carry

        lax.fori_loop(0, planes, body, 0)

    for place in range(planes):
        for group in range(groups):
            first_row = ((place // 4) * groups + group) * 8
            cells = gathered[pl.ds(5 * first_row + place % 4, 8, stride=5), :] + offset
            here = pl.ds((place * groups + group) * 8, 8)
            rhs[here, :] = cells
            coarse[here, :] = jnp.where(plane == (place & 1), cells * (-spacing_sq * SIXTH), 0.0)
    coarse_relax(1)

    def defect_pair(step, carry):
        for group in range(groups):
            total = jnp.zeros((8, 128), jnp.float32)
            for part in range(2):
                place = 2 * step + part
                centre, total_sum = tile_sum(place, group)
                total += rhs[tile(place, group), :] - (total_sum - 6.0 * centre) * (1.0 / spacing_sq)
            stage[tile(step, group), :] = total
        return carry

    half = planes // 2
    lines = half * groups
    for copy in copies[:5]:
        copy.wait()
    lax.fori_loop(0, half, defect_pair, 0)
    modes = jnp.zeros((lines, 256), jnp.float32)
    for part in range(8):
        modes += dot(stage[pl.ds(part, lines, stride=8), :], to_line[128 * part : 128 * part + 128, :])
    modes = jnp.concatenate([modes[:, :128], modes[:, 128:]], 0)
    modes = dot(from_plane[...], dot(to_plane[...], modes) * inverse[...])
    modes = jnp.concatenate([modes[:lines], modes[lines:]], 1)
    for part in range(8):
        stage[pl.ds(part, lines, stride=8), :] = dot(modes, from_line[:, 128 * part : 128 * part + 128])

    def add_back(step, carry):
        for group in range(groups):
            correction = stage[tile(step, group), :]
            for part in range(2):
                coarse[tile(2 * step + part, group), :] += correction
        return carry

    lax.fori_loop(0, half, add_back, 0)
    coarse_relax(0)
    coarse_relax(1)

    my_x, my_y, my_z = where_ref[0], where_ref[1], where_ref[2]
    for number, along_y in enumerate((0, 1, groups - 1)):
        for row, along_x in enumerate((0, 1, 2, 3, 4, 5, planes - 2, planes - 1)):
            for column, along_z in enumerate((0, 1, 7)):
                place = lax.rem(4 * my_x + along_x, planes)
                group = lax.rem(my_y + along_y, groups)
                line = lax.rem(my_z + along_z, 8)
                chosen[8 * number + row : 8 * number + row + 1, 128 * column : 128 * column + 128] = coarse[
                    pl.ds((place * groups + group) * 8 + line, 1), :
                ]
    for copy in copies[5:15]:
        copy.wait()
    picked = dot(chosen[...], pick[...])
    for number, line, slot in ((0, 0, 0), (0, 1, 2), (0, 2, 4), (0, 3, 6), (1, 0, 8), (1, 1, 10), (2, 2, 20), (2, 3, 22)):
        rows = picked[8 * number : 8 * number + 8, 128 * line : 128 * line + 128]
        for part in range(2):
            for twice in range(2):
                extra[pl.ds(24 * part + slot + twice, 8, stride=48), :] = rows

    sides = jnp.concatenate([z_right[...], z_left[...]], 0)
    beside = dot(sides, place_one[...], ((0,), (0,))).reshape(16, 16, 128)
    line_one = lax.broadcasted_iota(jnp.int32, (24, 128), 0)
    lane_one = lax.broadcasted_iota(jnp.int32, (24, 128), 1)
    plane_one = (line_one + lane_one) & 1
    from_z = jnp.logical_and(lane_one >= 64, jnp.logical_or(line_one < 10, line_one >= 22))
    for place in range(24):
        if place < 10 or place >= 22:
            row = place if place < 10 else place - 8
            cells = jnp.concatenate([one_own[row, :8], y_right[row], y_left[row]], 0)
            sideways = beside[row]
            cells = jnp.where(from_z, jnp.concatenate([sideways, sideways[8:]], 0), cells)
        elif place < 13 or place >= 19:
            cells = x_right[place - 8] if place < 13 else x_left[place - 16]
            cells = jnp.concatenate([cells, cells[8:]], 0)
        else:
            cells = jnp.zeros((24, 128), jnp.float32)
        cells = cells + offset
        one_rhs[place] = cells
        one[place] = jnp.where(plane_one == (place & 1), cells * (-4.0 * SIXTH), 0.0)
    relax(one, lambda place: one_rhs[place], 4.0, 1, -4, 16)
    for row in range(16):
        place = row if row < 12 else row + 8
        one[place] += extra[24 * row : 24 * row + 24, :]
    relax(one, lambda place: one_rhs[place], 4.0, 0, -3, 14)
    relax(one, lambda place: one_rhs[place], 4.0, 1, -2, 12)

    wide = jnp.concatenate([one[0:10], one[22:24]], 0).reshape(288, 128)
    wide = dot(wide, refine_z[...])
    for row in range(12):
        for part, fine in ((0, fine_low), (1, fine_high)):
            cells = wide[24 * row : 24 * row + 24, 128 * part : 128 * part + 128]
            for twice in range(2):
                fine[pl.ds(32 * row + twice, 8, stride=2), :] = cells[:8]
                fine[pl.ds(32 * row + 16 + twice, 4, stride=2), :] = cells[8:12]
                fine[pl.ds(32 * row + 24 + twice, 4, stride=2), :] = cells[20:24]
    plane_fine = parity_plane((32, 256))
    for copy in copies[15:]:
        copy.wait()
    for place in tuple(range(20)) + tuple(range(28, 32)):
        row = place // 2 if place < 20 else place // 2 - 4
        lift = jnp.concatenate([fine_low[32 * row : 32 * row + 32, :], fine_high[32 * row : 32 * row + 32, :]], 1)
        moved = jnp.where(plane_fine == (place & 1), offset * (-SIXTH), offset * (-2.0 * SIXTH))
        work[place] = values[place] + (lift + moved)
    extent = potential_out.shape[0]
    relax(work, lambda place: source[place] + offset, 1.0, 0, -2, extent + 4)
    relax(work, lambda place: source[place] + offset, 1.0, 1, -1, extent + 2)

    def finish(place, carry):
        cells = work[place]
        after, before = work[lax.rem(place + 1, 32)], work[lax.rem(place + 31, 32)]
        along_x = (after[:16, :128] - before[:16, :128]) * 0.5
        along_y = ((turn(cells, -1, 0) - turn(cells, 1, 0)) * 0.5)[:16, :128]
        along_z = ((turn(cells, -1, 1) - turn(cells, 1, 1)) * 0.5)[:16, :128]
        potential_out[place] = cells[:16, :128]
        density = conserved[0, place]
        first, second, third = conserved[1, place], conserved[2, place], conserved[3, place]
        energy_source = first * along_x + second * along_y + third * along_z
        updated[0, place] = density + step_size * update[0, place]
        updated[1, place] = first + step_size * (update[1, place] - density * along_x)
        updated[2, place] = second + step_size * (update[2, place] - density * along_y)
        updated[3, place] = third + step_size * (update[3, place] - density * along_z)
        updated[4, place] = conserved[4, place] + step_size * (update[4, place] - energy_source)
        return carry

    lax.fori_loop(0, extent, finish, 0, unroll=2)


def flux_x_kernel(fluid, left, right, out, states, fluxes):
    extent = fluid.shape[1]

    def fill(place, cells):
        for member, values in enumerate(primitives(*cells)):
            states[place, member] = values

    for row in range(2):
        for place, arrived, at in ((row, left, 2 * WIDE - 2 + row), (extent + 2 + row, right, WIDE + row)):
            fill(place, [arrived[at]] + [arrived[2 * WIDE + 2 * part + row] for part in range(4)])

    def own(place, carry):
        fill(place + 2, [fluid[member, place] for member in range(5)])
        return carry

    def face(place, carry):
        around = [[states[place + step, member] for member in range(5)] for step in range(4)]
        for member, values in enumerate(face_flux(*around, 0)):
            fluxes[place, member] = values
        return carry

    def difference(place, carry):
        for member in range(5):
            out[member, place] = fluxes[place, member] - fluxes[place + 1, member]
        return carry

    lax.fori_loop(0, extent, own, 0, unroll=2)
    lax.fori_loop(0, extent + 1, face, 0)
    lax.fori_loop(0, extent, difference, 0)


def flux_y_kernel(fluid, left, right, part, out, beside):
    extent = fluid.shape[1]
    lines = extent + 2 * WIDE
    row = lax.broadcasted_iota(jnp.int32, (8, 128), 0)
    for member in range(4):
        for line in range(2):
            place = 2 * lines + 2 * (2 * member + line)
            beside.at[member][pl.ds(line, extent, stride=8), :] = right[place : place + 2].reshape(16, 128)
            beside.at[member][pl.ds(6 + line, extent, stride=8), :] = left[place : place + 2].reshape(16, 128)

    def slab(place, carry):
        far = jnp.where(row < 4, right[lines + place], left[lines + place])
        cells = [jnp.concatenate([fluid[0, place], far], 0)]
        for member in range(4):
            far = beside[member, pl.ds(pl.multiple_of(8 * place, 8), 8), :]
            cells.append(jnp.concatenate([fluid[1 + member, place], far], 0))
        state = primitives(*cells)
        around = [[turn(values, -step, 0) for values in state] for step in (-1, 0, 1, 2)]
        for member, values in enumerate(face_flux(around[0], state, around[2], around[3], 1)):
            out[member, place] = part[member, place] + (turn(values, 1, 0) - values)[:16]
        return carry

    lax.fori_loop(0, extent, slab, 0)


def flux_z_kernel(fluid, left, right, ends, part, out, thin, beside):
    extent = fluid.shape[1]
    lines = extent + 2 * WIDE
    for start, count, ref in ((32 * lines, 32 * extent, thin), (64 * lines, 64 * extent, beside)):
        sides = jnp.concatenate([right[:, start : start + count], left[:, start : start + count]], 0)
        ref[...] = dot(sides, ends[...], ((0,), (0,)))

    def slab(place, carry):
        far = thin[pl.ds(pl.multiple_of(32 * place, 32), 16), :]
        cells = [jnp.concatenate([fluid[0, place], far], 1)]
        for member in range(4):
            far = beside[pl.ds(pl.multiple_of(16 * extent * member + 16 * place, 16), 16), :]
            cells.append(jnp.concatenate([fluid[1 + member, place], far], 1))
        state = primitives(*cells)
        around = [[turn(values, -step, 1) for values in state] for step in (-1, 0, 1, 2)]
        for member, values in enumerate(face_flux(around[0], state, around[2], around[3], 2)):
            out[member, place] = part[member, place] + (turn(values, 1, 1) - values)[:, :128]
        return carry

    lax.fori_loop(0, extent, slab, 0)


def call(kernel, shapes, scratch=(), operands=None, late=0):
    extra = {}
    if late:
        results = [pl.BlockSpec(memory_space=pl.ANY if number < late else pltpu.VMEM) for number in range(len(shapes))]
        extra = dict(out_specs=results)
    if operands is not None:
        specs = [pl.BlockSpec(shape, functools.partial(lambda rank, step: (0,) * rank, len(shape))) for shape in operands]
        results = [pl.BlockSpec(shape, functools.partial(lambda rank, step: (0,) * rank, len(shape))) for shape in shapes]
        extra = dict(grid=(1,), in_specs=specs, out_specs=results)
    return pl.pallas_call(
        kernel,
        **extra,
        out_shape=[jax.ShapeDtypeStruct(shape, jnp.float32) for shape in shapes],
        scratch_shapes=[pltpu.VMEM(shape, jnp.float32) for shape in scratch]
        + ([pltpu.SemaphoreType.DMA((late,))] if late else []),
        compiler_params=SMALL,
    )


def halved(fine):
    return np.repeat(np.eye(fine // 2, dtype=np.float32), 2, 0)


def shards(conserved, potential):
    cells_x, cells_y, cells_z = potential.shape
    count_x, count_y, count_z = (lax.axis_size(axis) for axis in AXES)
    devices = count_x * count_y * count_z
    lines = cells_x + 2 * WIDE
    block, whole, flat = (cells_x, cells_y, cells_z), conserved.shape, (5, cells_x * cells_y, cells_z)
    side, slab, ends = (2 * WIDE + 8, cells_y, cells_z), (2 * lines + 16, 8, cells_z), end_columns(cells_z, WIDE)
    fluid_rows = conserved.reshape(flat)

    head, tail = call(pack_x_kernel, [side] * 2, (), [block, whole])(potential, conserved)
    x_left, x_right = shift(tail, "gx", 1), shift(head, "gx", -1)
    head, tail = call(pack_y_kernel, [slab] * 2, (), [block, (1,) + block, flat, side, side])(
        potential, conserved, fluid_rows, x_left, x_right
    )
    y_left, y_right = shift(tail, "gy", 1), shift(head, "gy", -1)
    fluid, *sides, head, tail = lax.optimization_barrier((conserved, x_left, x_right, head, tail))
    update = call(flux_x_kernel, [whole], [(cells_x + 4, 5) + block[1:], (cells_x + 1, 5) + block[1:]])(fluid, *sides)[0]
    y_left, y_right, update = lax.optimization_barrier((y_left, y_right, update))
    columns = (8, 64 * lines + 4 * cells_x * cells_y)
    main, head, tail = call(
        pack_z_kernel,
        [(2 * lines, 32, cells_z), columns, columns],
        (),
        [block, (1,) + block, flat, side, side, slab, slab, ends.shape],
    )(potential, conserved, fluid_rows, x_left, x_right, y_left, y_right, ends)
    z_left, z_right = shift(tail, "gz", 1), shift(head, "gz", -1)
    fluid, *sides, update, head = lax.optimization_barrier((conserved, y_left, y_right, update, head))
    update = call(flux_y_kernel, [whole], [(4, 8 * cells_x, cells_z)])(fluid, *sides, update)[0]
    z_left, z_right, update = lax.optimization_barrier((z_left, z_right, update))

    pair_two = np.zeros((4, 128, 4, 32), np.float32)
    for part in range(4):
        pair_two[part, :64, part] = 0.125 * halved(64)
    window = (32, 32, 2 * cells_z)
    sizes = [window, window, (16, 16, 128), (8, 16, 128), (16, 8, 128), (8, 256), (8, 256), (devices * 5, 128)]
    tables = (0.125 * halved(256), pair_two.reshape(512, 128))
    values, source, one, one_x, one_y, one_head, one_tail, payload = call(
        pre_kernel,
        sizes,
        [window, window, (512, 256), (512, 128), (16, 16, 128), (64, 128)],
        late=2,
    )(main, z_left, z_right, ends, end_columns(64, 5), conserved, *tables)

    one_halo = [shift(one_x, "gx", 1), shift(one_x, "gx", -1), shift(one_y, "gy", 1), shift(one_y, "gy", -1)]
    one_halo.append(shift(one_tail, "gz", 1))
    gathered = lax.all_to_all(payload.reshape(devices, 1, 640), AXES, 0, 0, tiled=True).reshape(devices * 5, 128)

    fluid, update, *sides, _ = lax.optimization_barrier((conserved, update, z_left, z_right, payload))
    update = call(flux_z_kernel, [whole], [(32 * cells_x, cells_z), (64 * cells_x, cells_z)])(fluid, *sides, ends, update)[0]
    one_head, update = lax.optimization_barrier((one_head, update))
    one_halo.append(shift(one_head, "gz", -1))
    planes, groups = 4 * count_x, count_y
    position = jnp.stack([lax.axis_index(axis) for axis in AXES]).astype(jnp.int32)
    operands = (gathered, values, source, one, *one_halo, conserved, update)
    operands += coarse_tables(planes, groups, 64.0) + (pick_table(), place_columns(64, 5), halved(256).T)
    order = (12, 13, 14, 15, 16, 17, 3, 4, 5, 6, 7, 8, 9, 18, 19, 1, 2, 10, 11)
    tiles = planes * groups * 8
    updated, potential_out = pl.pallas_call(
        functools.partial(post_kernel, planes, groups, float(devices * cells_x * cells_y * cells_z)),
        out_shape=[jax.ShapeDtypeStruct(array.shape, jnp.float32) for array in (conserved, potential)],
        in_specs=[pl.BlockSpec(memory_space=pltpu.SMEM)]
        + [pl.BlockSpec(memory_space=pl.ANY if number else pltpu.VMEM) for number in range(len(operands))],
        scratch_shapes=[
            pltpu.VMEM(shape, jnp.float32)
            for shape in (
                (tiles + 8, 128), (tiles, 128), (tiles // 2, 128), (24, 384), (384, 128),
                (24, 24, 128), (24, 24, 128), (400, 128), (400, 128), (32, 32, 256),
            )
        ]
        + [pltpu.VMEM(operands[number].shape, jnp.float32) for number in order]
        + [pltpu.SemaphoreType.DMA((len(order),))],
        compiler_params=BIG,
    )(position, *operands)
    return (updated, potential_out)


def solution(mesh):
    in_specs = (P(None, "gx", "gy", "gz"), P("gx", "gy", "gz"))
    out_specs = (P(None, "gx", "gy", "gz"), P("gx", "gy", "gz"))
    return jax.shard_map(shards, mesh=mesh, in_specs=in_specs, out_specs=out_specs, check_vma=False)
```

```python
import functools

import numpy as np
import jax
import jax.numpy as jnp
from jax import lax
from jax.experimental import pallas as pl
from jax.experimental.pallas import tpu as pltpu
from jax.sharding import PartitionSpec as P

LEVELS = 3


gamma_gas = 5.0 / 3.0
courant = 0.4
coupling = 0.01


def primitives(density, first, second, third, energy):
    inverse = 1.0 / density
    kinetic = 0.5 * inverse * (first * first + second * second + third * third)
    pressure = (gamma_gas - 1.0) * (energy - kinetic)
    return [density, first * inverse, second * inverse, third * inverse, pressure]


def limited(first, second):
    return jnp.maximum(0.0, jnp.minimum(first, second)) + jnp.minimum(0.0, jnp.maximum(first, second))


def face_flux(before, centre, after_one, after_two, normal):
    lefts, rights = [], []
    for one, two, three, four in zip(before, centre, after_one, after_two):
        middle = three - two
        lefts.append(two + 0.5 * limited(two - one, middle))
        rights.append(three - 0.5 * limited(middle, four - three))
    along = 1 + normal
    others = [member for member in (1, 2, 3) if member != along]

    def unpack(state):
        density, speed, pressure = state[0], state[along], state[4]
        inverse = 1.0 / density
        squares = speed * speed + state[others[0]] * state[others[0]] + state[others[1]] * state[others[1]]
        energy = pressure * (1.0 / (gamma_gas - 1.0)) + 0.5 * density * squares
        return inverse, energy, jnp.sqrt(gamma_gas * pressure * inverse)

    left_inverse, left_energy, left_sound = unpack(lefts)
    right_inverse, right_energy, right_sound = unpack(rights)
    left_speed, right_speed = lefts[along], rights[along]
    low_wave = jnp.minimum(left_speed - left_sound, right_speed - right_sound)
    high_wave = jnp.maximum(left_speed + left_sound, right_speed + right_sound)
    left_mass = lefts[0] * (low_wave - left_speed)
    right_mass = rights[0] * (high_wave - right_speed)
    star_wave = (rights[4] - lefts[4] + left_mass * left_speed - right_mass * right_speed) / (left_mass - right_mass)
    from_left = jnp.logical_or(low_wave >= 0.0, star_wave >= 0.0)
    state = [jnp.where(from_left, one, two) for one, two in zip(lefts, rights)]
    inverse = jnp.where(from_left, left_inverse, right_inverse)
    energy = jnp.where(from_left, left_energy, right_energy)
    wave = jnp.where(from_left, low_wave, high_wave)
    rate = jnp.where(from_left, left_mass, right_mass)
    unstarred = jnp.where(from_left, -low_wave, high_wave) <= 0.0
    density, speed, pressure = state[0], state[along], state[4]
    carried = density * speed
    spread = 1.0 / (wave - star_wave)
    factor = rate * spread
    starred_energy = factor * (energy * inverse) + (star_wave - speed) * (factor * star_wave + pressure * spread)

    def jump(starred, stored):
        return jnp.where(unstarred, 0.0, wave * (starred - stored))

    mass_flux = carried + jump(factor, density)
    flux = [None] * 5
    flux[0] = mass_flux
    flux[along] = carried * speed + pressure + jump(factor * star_wave, carried)
    for member in others:
        flux[member] = state[member] * mass_flux
    flux[4] = speed * (energy + pressure) + jump(starred_energy, energy)
    return flux


AXES = ("gx", "gy", "gz")
EXACT = lax.Precision.HIGHEST
SIXTH = 1.0 / 6.0
SMALL = pltpu.CompilerParams(vmem_limit_bytes=20 * 1024 * 1024)
PRE = pltpu.CompilerParams(vmem_limit_bytes=60 * 1024 * 1024)
BIG = pltpu.CompilerParams(vmem_limit_bytes=56 * 1024 * 1024)


def shift(payload, axis, step):
    count = lax.axis_size(axis)
    return lax.ppermute(payload, axis, [(i, (i + step) % count) for i in range(count)])


def dot(left, right, dims=((1,), (0,))):
    return lax.dot_general(left, right, (dims, ((), ())), precision=EXACT, preferred_element_type=jnp.float32)


def turn(values, step, axis):
    return pltpu.roll(values, step % values.shape[axis], axis)


def plane_sum(cells):
    total_sum = turn(cells, -1, 0) + turn(cells, 1, 0)
    return total_sum + turn(cells, -1, 1) + turn(cells, 1, 1)


def parity_plane(shape):
    return (lax.broadcasted_iota(jnp.int32, shape, 0) + lax.broadcasted_iota(jnp.int32, shape, 1)) & 1


def slab_sum(ref, place):
    count = ref.shape[0]
    return ref[lax.rem(place + 1, count)] + ref[lax.rem(place + count - 1, count)] + plane_sum(ref[place])


def relax(ref, source_of, spacing_sq, colour, first, count):
    extent = ref.shape[0]
    plane = parity_plane(ref.shape[1:])

    def body(step, carry):
        places = [lax.rem(4 * step + part + (first % extent), extent) for part in range(4)]
        fresh = []
        for place in places:
            renewed = (slab_sum(ref, place) - spacing_sq * source_of(place)) * SIXTH
            fresh.append(jnp.where(plane == ((colour + place) & 1), renewed, ref[place]))
        for place, cells in zip(places, fresh):
            ref[place] = cells
        return carry

    lax.fori_loop(0, (count + 3) // 4, body, 0)


WIDE = 7


def end_columns(extent, width):
    table = np.zeros((16, 128), np.float32)
    table[np.arange(width), np.arange(width)] = 1.0
    table[8 + np.arange(width), extent - width + np.arange(width)] = 1.0
    return table


def place_columns(extent, width):
    table = np.zeros((16, 128), np.float32)
    table[np.arange(width), (extent + np.arange(width)) % 128] = 1.0
    table[8 + np.arange(width), 128 - width + np.arange(width)] = 1.0
    return table


def pack_x_kernel(phi, fluid, head, tail):
    extent = phi.shape[0]
    for start, flow_start, out in ((0, 0, head), (extent - WIDE, extent - 2, tail)):
        out[:WIDE] = phi[start : start + WIDE]
        out[WIDE : 2 * WIDE] = fluid[0, start : start + WIDE]
        for part in range(4):
            out[2 * WIDE + 2 * part : 2 * WIDE + 2 * part + 2] = fluid[1 + part, flow_start : flow_start + 2]


def pack_y_kernel(phi, fluid, flat, left, right, head, tail):
    extent = phi.shape[0]
    lines = extent + 2 * WIDE
    for number, own in ((0, phi), (1, fluid.at[0])):
        base = number * lines
        arrived = pl.ds(number * WIDE, WIDE)
        for rows, out in ((pl.ds(0, 8), head), (pl.ds(8, 8), tail)):
            out[pl.ds(base, extent)] = own[:, rows]
            out[pl.ds(base + extent, WIDE)] = right[arrived, rows]
            out[pl.ds(base + extent + WIDE, WIDE)] = left[arrived, rows]
    for start, out in ((0, head), (14, tail)):
        for part in range(4):
            for row in range(2):
                place = 2 * lines + 2 * (2 * part + row)
                cells = flat.at[1 + part][pl.ds(start + row, extent, stride=16), :]
                out[place : place + 2] = cells.reshape(2, 8, 128)


def pack_z_kernel(phi, fluid, flat, x_left, x_right, y_left, y_right, ends, main, head, tail):
    extent = phi.shape[0]
    lines = extent + 2 * WIDE
    for number, own in ((0, phi), (1, fluid.at[0])):
        base = number * lines
        arrived = pl.ds(number * WIDE, WIDE)
        main[pl.ds(base, extent), :16] = own[...]
        main[pl.ds(base + extent, WIDE), :16] = x_right[arrived]
        main[pl.ds(base + extent + WIDE, WIDE), :16] = x_left[arrived]
        main[pl.ds(base, lines), 16:24] = y_right[pl.ds(base, lines)]
        main[pl.ds(base, lines), 24:] = y_left[pl.ds(base, lines)]
    columns = dot(ends[...], main[...].reshape(2 * lines * 32, 128), ((1,), (1,)))
    head[:, : 64 * lines] = columns[:8]
    tail[:, : 64 * lines] = columns[8:]
    columns = dot(ends[...], flat[1:].reshape(4 * flat.shape[1], 128), ((1,), (1,)))
    head[:, 64 * lines :] = columns[:8]
    tail[:, 64 * lines :] = columns[8:]


def pre_kernel(
    main, z_left, z_right, ends, ends_one, conserved, pair_z, pair_two,
    values_out, source_out, one, one_x, one_y, one_head, one_tail, payload,
    values, source, sums, halves, swept, rows, leaving,
):
    lines = main.shape[0] // 2
    extent = lines - 2 * WIDE
    sides = jnp.concatenate([z_right[:, : 64 * lines], z_left[:, : 64 * lines]], 0)
    beside = dot(sides, ends[...], ((0,), (0,))).reshape(2 * lines, 32, 128)
    for number, ref, scale in ((0, values, None), (1, source, coupling)):
        base = number * lines
        gap = extent + WIDE
        ref[gap : 32 - WIDE] = jnp.zeros((32 - WIDE - gap, 32, 256), jnp.float32)
        for cells, columns in ((main, slice(0, 128)), (beside, slice(128, 256))):
            upper = cells[base : base + gap]
            lower = cells[base + gap : base + lines]
            ref[:gap, :, columns] = upper if scale is None else scale * upper
            ref[32 - WIDE :, :, columns] = lower if scale is None else scale * lower

    source_copy = pltpu.make_async_copy(source, source_out, leaving.at[0])
    source_copy.start()
    relax(values, lambda place: source[place], 1.0, 0, -6, extent + 12)
    relax(values, lambda place: source[place], 1.0, 1, -5, extent + 10)
    values_copy = pltpu.make_async_copy(values, values_out, leaving.at[1])
    values_copy.start()

    sums[10 * 32 : 14 * 32, :] = jnp.zeros((4 * 32, 256), jnp.float32)

    def defect_pair(turned, carry):
        step = lax.rem(turned + 14, 16)
        total_sum = jnp.zeros((32, 256), jnp.float32)
        for part in range(2):
            place = 2 * step + part
            total_sum += source[place] - (slab_sum(values, place) - 6.0 * values[place])
        sums[pl.ds(pl.multiple_of(step * 32, 32), 32), :] = total_sum
        return carry

    lax.fori_loop(0, 12, defect_pair, 0, unroll=2)
    halves[...] = dot(sums[...], pair_z[...])
    one[...] = (halves[pl.ds(0, 256, stride=2), :] + halves[pl.ds(1, 256, stride=2), :]).reshape(16, 16, 128)
    one_x[...] = one[:8]
    one_y[...] = one[:, :8]
    columns = dot(ends_one[...], one[...].reshape(256, 128), ((1,), (1,)))
    one_head[...] = columns[:8]
    one_tail[...] = columns[8:]

    plane = parity_plane((16, 128))
    for place in range(16):
        swept[place] = jnp.where(plane == (place & 1), one[place] * (-4.0 * SIXTH), 0.0)
    relax(swept, lambda place: one[place], 4.0, 1, 0, 16)
    for step in range(8):
        total_sum = jnp.zeros((16, 128), jnp.float32)
        for part in range(2):
            place = 2 * step + part
            total_sum += one[place] - (slab_sum(swept, place) - 6.0 * swept[place]) * 0.25
        rows[8 * step : 8 * step + 8, :] = total_sum[:8]
    packed = jnp.zeros((8, 128), jnp.float32)
    for part in range(4):
        both = rows[pl.ds(2 * part, 8, stride=8), :] + rows[pl.ds(2 * part + 1, 8, stride=8), :]
        packed += dot(both, pair_two[128 * part : 128 * part + 128, :])

    def measure_slab(place, carry):
        mass, speed = carry
        density = conserved[0, place]
        inverse = 1.0 / density
        first, second, third = conserved[1, place], conserved[2, place], conserved[3, place]
        kinetic = 0.5 * inverse * (first * first + second * second + third * third)
        pressure = (gamma_gas - 1.0) * (conserved[4, place] - kinetic)
        signal = (jnp.abs(first) + jnp.abs(second) + jnp.abs(third)) * inverse
        signal += 3.0 * jnp.sqrt(gamma_gas * pressure * inverse)
        return mass + density, jnp.maximum(speed, signal)

    blank = jnp.zeros((16, 128), jnp.float32)
    mass, speed = lax.fori_loop(0, extent, measure_slab, (blank, blank), unroll=2)
    mass = jnp.sum(jnp.sum(mass, axis=0, keepdims=True), axis=1, keepdims=True)
    speed = jnp.max(jnp.max(speed, axis=0, keepdims=True), axis=1, keepdims=True)
    lane = lax.broadcasted_iota(jnp.int32, (1, 128), 1)
    extra = jnp.where(lane == 0, mass, jnp.where(lane == 1, speed, 0.0))
    count = payload.shape[0] // 5
    for part in range(4):
        payload[pl.ds(part, count, stride=5), :] = jnp.broadcast_to(packed[part : part + 1], (count, 128))
    payload[pl.ds(4, count, stride=5), :] = jnp.broadcast_to(extra, (count, 128))
    source_copy.wait()
    values_copy.wait()


def cas(extent):
    angle = 2.0 * np.pi / extent * np.outer(np.arange(extent), np.arange(extent))
    return (np.cos(angle) + np.sin(angle)) / np.sqrt(extent)


def eigen(extent, spacing_sq):
    return (2.0 * np.cos(2.0 * np.pi / extent * np.arange(extent)) - 2.0) / spacing_sq


def coarse_tables(planes, groups, spacing_sq):
    half = planes // 2
    line = cas(128)
    same = np.repeat(np.eye(2), 2, 0)
    spread = np.repeat(line, 2, 0).reshape(8, 32, 128)
    forward = np.einsum("ab,gzk->gazbk", same, spread).reshape(1024, 256)
    across = cas(2 * groups).reshape(2 * groups, groups, 2)
    plane = np.einsum("px,qgb->pqbxg", cas(half), across).reshape(2 * groups * half, 2 * groups * half)
    total = (eigen(half, spacing_sq)[:, None] + eigen(2 * groups, spacing_sq)).reshape(-1, 1) + eigen(128, spacing_sq)
    total[0, 0] = 1.0
    inverse = 1.0 / total
    inverse[0, 0] = 0.0
    tables = (0.125 * forward, plane, inverse, plane.T, forward.T)
    return tuple(np.ascontiguousarray(table, dtype=np.float32) for table in tables)


def pick_table():
    table = np.zeros((3, 4, 32, 4, 128), np.float32)
    for line in range(4):
        for cell in range(32):
            table[0, line, cell, line, 2 * cell : 2 * cell + 2] = 1.0
        for cell in range(2):
            table[1, line, cell, line, 64 + 2 * cell : 66 + 2 * cell] = 1.0
            table[2, line, 30 + cell, line, 124 + 2 * cell : 126 + 2 * cell] = 1.0
    return table.reshape(384, 512)


def post_kernel(
    planes, groups, cells_total,
    where_ref, gathered, values, source, one_own, x_left, x_right, y_left, y_right, z_left, z_right, conserved, update,
    to_line, to_plane, inverse, from_plane, from_line, pick, place_one, refine_z,
    updated, potential_out,
    coarse, rhs, stage, chosen, extra, one_rhs, one, fine_low, fine_high, work,
    *held,
):
    far = (to_line, to_plane, inverse, from_plane, from_line, pick, one_own, x_left, x_right, y_left, y_right, z_left, z_right)
    far += (place_one, refine_z, values, source, conserved, update)
    arrivals = held[-1]
    copies = [pltpu.make_async_copy(ref, near, arrivals.at[number]) for number, (ref, near) in enumerate(zip(far, held))]
    for copy in copies:
        copy.start()
    to_line, to_plane, inverse, from_plane, from_line, pick, one_own, x_left, x_right, y_left, y_right, z_left, z_right = held[:13]
    place_one, refine_z, values, source, conserved, update = held[13:-1]

    last = gathered[pl.ds(4, gathered.shape[0] // 5, stride=5), :]
    lane_row = lax.broadcasted_iota(jnp.int32, (1, 128), 1)
    mass = jnp.sum(jnp.where(lane_row == 0, jnp.sum(last, axis=0, keepdims=True), 0.0), axis=1, keepdims=True)
    speed = jnp.sum(jnp.where(lane_row == 1, jnp.max(last, axis=0, keepdims=True), 0.0), axis=1, keepdims=True)
    offset = mass * (-coupling / cells_total)
    step_size = courant / speed

    spacing_sq = 16.0
    lane = lax.broadcasted_iota(jnp.int32, (8, 128), 1)
    cell = lane & 31
    plane = (cell + (lane >> 5)) & 1

    def tile(place, group):
        return pl.ds(pl.multiple_of((place * groups + group) * 8, 8), 8)

    def tile_sum(place, group):
        centre = coarse[tile(place, group), :]
        total_sum = coarse[tile(lax.rem(place + 1, planes), group), :]
        total_sum += coarse[tile(lax.rem(place + planes - 1, planes), group), :]
        after = coarse[tile(place, (group + 1) % groups), :]
        before = coarse[tile(place, (group + groups - 1) % groups), :]
        total_sum += turn(jnp.where(lane < 32, after, centre), -32, 1)
        total_sum += turn(jnp.where(lane >= 96, before, centre), 32, 1)
        total_sum += jnp.where(cell == 31, turn(turn(centre, -1, 0), 31, 1), turn(centre, -1, 1))
        total_sum += jnp.where(cell == 0, turn(turn(centre, 1, 0), -31, 1), turn(centre, 1, 1))
        return centre, total_sum

    def coarse_relax(colour):
        def body(step, carry):
            tiles = [(2 * step + part, group) for part in range(2) for group in range(groups)]
            fresh = []
            for place, group in tiles:
                centre, total_sum = tile_sum(place, group)
                renewed = (total_sum - spacing_sq * rhs[tile(place, group), :]) * SIXTH
                fresh.append(jnp.where(plane == ((colour + place) & 1), renewed, centre))
            for (place, group), cells in zip(tiles, fresh):
                coarse[tile(place, group), :] = cells
            return carry

        lax.fori_loop(0, planes // 2, body, 0)

    for place in range(planes):
        for group in range(groups):
            first_row = ((place // 4) * groups + group) * 8
            cells = gathered[pl.ds(5 * first_row + place % 4, 8, stride=5), :] + offset
            here = pl.ds((place * groups + group) * 8, 8)
            rhs[here, :] = cells
            coarse[here, :] = jnp.where(plane == (place & 1), cells * (-spacing_sq * SIXTH), 0.0)
    coarse_relax(1)

    def defect_pair(step, carry):
        for group in range(groups):
            total = jnp.zeros((8, 128), jnp.float32)
            for part in range(2):
                place = 2 * step + part
                centre, total_sum = tile_sum(place, group)
                total += rhs[tile(place, group), :] - (total_sum - 6.0 * centre) * (1.0 / spacing_sq)
            stage[tile(step, group), :] = total
        return carry

    half = planes // 2
    lines = half * groups
    for copy in copies[:5]:
        copy.wait()
    lax.fori_loop(0, half, defect_pair, 0)
    modes = jnp.zeros((lines, 256), jnp.float32)
    for part in range(8):
        modes += dot(stage[pl.ds(part, lines, stride=8), :], to_line[128 * part : 128 * part + 128, :])
    modes = jnp.concatenate([modes[:, :128], modes[:, 128:]], 0)
    modes = dot(from_plane[...], dot(to_plane[...], modes) * inverse[...])
    modes = jnp.concatenate([modes[:lines], modes[lines:]], 1)
    for part in range(8):
        stage[pl.ds(part, lines, stride=8), :] = dot(modes, from_line[:, 128 * part : 128 * part + 128])

    def add_back(step, carry):
        for group in range(groups):
            correction = stage[tile(step, group), :]
            for part in range(2):
                coarse[tile(2 * step + part, group), :] += correction
        return carry

    lax.fori_loop(0, half, add_back, 0)
    coarse_relax(0)
    coarse_relax(1)

    my_x, my_y, my_z = where_ref[0], where_ref[1], where_ref[2]
    for number, along_y in enumerate((0, 1, groups - 1)):
        for row, along_x in enumerate((0, 1, 2, 3, 4, 5, planes - 2, planes - 1)):
            for column, along_z in enumerate((0, 1, 7)):
                place = lax.rem(4 * my_x + along_x, planes)
                group = lax.rem(my_y + along_y, groups)
                line = lax.rem(my_z + along_z, 8)
                chosen[8 * number + row : 8 * number + row + 1, 128 * column : 128 * column + 128] = coarse[
                    pl.ds((place * groups + group) * 8 + line, 1), :
                ]
    for copy in copies[5:15]:
        copy.wait()
    picked = dot(chosen[...], pick[...])
    for number, line, slot in ((0, 0, 0), (0, 1, 2), (0, 2, 4), (0, 3, 6), (1, 0, 8), (1, 1, 10), (2, 2, 20), (2, 3, 22)):
        rows = picked[8 * number : 8 * number + 8, 128 * line : 128 * line + 128]
        for part in range(2):
            for twice in range(2):
                extra[pl.ds(24 * part + slot + twice, 8, stride=48), :] = rows

    sides = jnp.concatenate([z_right[...], z_left[...]], 0)
    beside = dot(sides, place_one[...], ((0,), (0,))).reshape(16, 16, 128)
    line_one = lax.broadcasted_iota(jnp.int32, (24, 128), 0)
    lane_one = lax.broadcasted_iota(jnp.int32, (24, 128), 1)
    plane_one = (line_one + lane_one) & 1
    from_z = jnp.logical_and(lane_one >= 64, jnp.logical_or(line_one < 10, line_one >= 22))
    for place in range(24):
        if place < 10 or place >= 22:
            row = place if place < 10 else place - 8
            cells = jnp.concatenate([one_own[row, :8], y_right[row], y_left[row]], 0)
            sideways = beside[row]
            cells = jnp.where(from_z, jnp.concatenate([sideways, sideways[8:]], 0), cells)
        elif place < 13 or place >= 19:
            cells = x_right[place - 8] if place < 13 else x_left[place - 16]
            cells = jnp.concatenate([cells, cells[8:]], 0)
        else:
            cells = jnp.zeros((24, 128), jnp.float32)
        cells = cells + offset
        one_rhs[place] = cells
        one[place] = jnp.where(plane_one == (place & 1), cells * (-4.0 * SIXTH), 0.0)
    relax(one, lambda place: one_rhs[place], 4.0, 1, -4, 16)
    for row in range(16):
        place = row if row < 12 else row + 8
        one[place] += extra[24 * row : 24 * row + 24, :]
    relax(one, lambda place: one_rhs[place], 4.0, 0, -3, 14)
    relax(one, lambda place: one_rhs[place], 4.0, 1, -2, 12)

    wide = jnp.concatenate([one[0:10], one[22:24]], 0).reshape(288, 128)
    wide = dot(wide, refine_z[...])
    for row in range(12):
        for part, fine in ((0, fine_low), (1, fine_high)):
            cells = wide[24 * row : 24 * row + 24, 128 * part : 128 * part + 128]
            for twice in range(2):
                fine[pl.ds(32 * row + twice, 8, stride=2), :] = cells[:8]
                fine[pl.ds(32 * row + 16 + twice, 4, stride=2), :] = cells[8:12]
                fine[pl.ds(32 * row + 24 + twice, 4, stride=2), :] = cells[20:24]
    plane_fine = parity_plane((32, 256))
    for copy in copies[15:]:
        copy.wait()
    for place in tuple(range(20)) + tuple(range(28, 32)):
        row = place // 2 if place < 20 else place // 2 - 4
        lift = jnp.concatenate([fine_low[32 * row : 32 * row + 32, :], fine_high[32 * row : 32 * row + 32, :]], 1)
        moved = jnp.where(plane_fine == (place & 1), offset * (-SIXTH), offset * (-2.0 * SIXTH))
        work[place] = values[place] + (lift + moved)
    extent = potential_out.shape[0]
    relax(work, lambda place: source[place] + offset, 1.0, 0, -2, extent + 4)
    relax(work, lambda place: source[place] + offset, 1.0, 1, -1, extent + 2)

    def finish(place, carry):
        cells = work[place]
        after, before = work[lax.rem(place + 1, 32)], work[lax.rem(place + 31, 32)]
        along_x = (after[:16, :128] - before[:16, :128]) * 0.5
        along_y = ((turn(cells, -1, 0) - turn(cells, 1, 0)) * 0.5)[:16, :128]
        along_z = ((turn(cells, -1, 1) - turn(cells, 1, 1)) * 0.5)[:16, :128]
        potential_out[place] = cells[:16, :128]
        density = conserved[0, place]
        first, second, third = conserved[1, place], conserved[2, place], conserved[3, place]
        energy_source = first * along_x + second * along_y + third * along_z
        updated[0, place] = density + step_size * update[0, place]
        updated[1, place] = first + step_size * (update[1, place] - density * along_x)
        updated[2, place] = second + step_size * (update[2, place] - density * along_y)
        updated[3, place] = third + step_size * (update[3, place] - density * along_z)
        updated[4, place] = conserved[4, place] + step_size * (update[4, place] - energy_source)
        return carry

    lax.fori_loop(0, extent, finish, 0, unroll=2)


def flux_x_kernel(fluid, left, right, out, states, fluxes):
    extent = fluid.shape[1]

    def fill(place, cells):
        for member, values in enumerate(primitives(*cells)):
            states[place, member] = values

    for row in range(2):
        for place, arrived, at in ((row, left, 2 * WIDE - 2 + row), (extent + 2 + row, right, WIDE + row)):
            fill(place, [arrived[at]] + [arrived[2 * WIDE + 2 * part + row] for part in range(4)])

    def own(place, carry):
        fill(place + 2, [fluid[member, place] for member in range(5)])
        return carry

    def face(place, carry):
        around = [[states[place + step, member] for member in range(5)] for step in range(4)]
        for member, values in enumerate(face_flux(*around, 0)):
            fluxes[place, member] = values
        return carry

    def difference(place, carry):
        for member in range(5):
            out[member, place] = fluxes[place, member] - fluxes[place + 1, member]
        return carry

    lax.fori_loop(0, extent, own, 0, unroll=2)
    lax.fori_loop(0, extent + 1, face, 0)
    lax.fori_loop(0, extent, difference, 0)


def flux_y_kernel(fluid, left, right, part, out, beside):
    extent = fluid.shape[1]
    lines = extent + 2 * WIDE
    row = lax.broadcasted_iota(jnp.int32, (8, 128), 0)
    for member in range(4):
        for line in range(2):
            place = 2 * lines + 2 * (2 * member + line)
            beside.at[member][pl.ds(line, extent, stride=8), :] = right[place : place + 2].reshape(16, 128)
            beside.at[member][pl.ds(6 + line, extent, stride=8), :] = left[place : place + 2].reshape(16, 128)

    def slab(place, carry):
        far = jnp.where(row < 4, right[lines + place], left[lines + place])
        cells = [jnp.concatenate([fluid[0, place], far], 0)]
        for member in range(4):
            far = beside[member, pl.ds(pl.multiple_of(8 * place, 8), 8), :]
            cells.append(jnp.concatenate([fluid[1 + member, place], far], 0))
        state = primitives(*cells)
        around = [[turn(values, -step, 0) for values in state] for step in (-1, 0, 1, 2)]
        for member, values in enumerate(face_flux(around[0], state, around[2], around[3], 1)):
            out[member, place] = part[member, place] + (turn(values, 1, 0) - values)[:16]
        return carry

    lax.fori_loop(0, extent, slab, 0)


def flux_z_kernel(fluid, left, right, ends, part, out, thin, beside):
    extent = fluid.shape[1]
    lines = extent + 2 * WIDE
    for start, count, ref in ((32 * lines, 32 * extent, thin), (64 * lines, 64 * extent, beside)):
        sides = jnp.concatenate([right[:, start : start + count], left[:, start : start + count]], 0)
        ref[...] = dot(sides, ends[...], ((0,), (0,)))

    def slab(place, carry):
        far = thin[pl.ds(pl.multiple_of(32 * place, 32), 16), :]
        cells = [jnp.concatenate([fluid[0, place], far], 1)]
        for member in range(4):
            far = beside[pl.ds(pl.multiple_of(16 * extent * member + 16 * place, 16), 16), :]
            cells.append(jnp.concatenate([fluid[1 + member, place], far], 1))
        state = primitives(*cells)
        around = [[turn(values, -step, 1) for values in state] for step in (-1, 0, 1, 2)]
        for member, values in enumerate(face_flux(around[0], state, around[2], around[3], 2)):
            out[member, place] = part[member, place] + (turn(values, 1, 1) - values)[:, :128]
        return carry

    lax.fori_loop(0, extent, slab, 0)


def call(kernel, shapes, scratch=(), operands=None, late=0):
    extra = {}
    if late:
        results = [pl.BlockSpec(memory_space=pl.ANY if number < late else pltpu.VMEM) for number in range(len(shapes))]
        extra = dict(out_specs=results)
    if operands is not None:
        specs = [pl.BlockSpec(shape, functools.partial(lambda rank, step: (0,) * rank, len(shape))) for shape in operands]
        results = [pl.BlockSpec(shape, functools.partial(lambda rank, step: (0,) * rank, len(shape))) for shape in shapes]
        extra = dict(grid=(1,), in_specs=specs, out_specs=results)
    return pl.pallas_call(
        kernel,
        **extra,
        out_shape=[jax.ShapeDtypeStruct(shape, jnp.float32) for shape in shapes],
        scratch_shapes=[pltpu.VMEM(shape, jnp.float32) for shape in scratch]
        + ([pltpu.SemaphoreType.DMA((late,))] if late else []),
        compiler_params=PRE if late else SMALL,
    )


def halved(fine):
    return np.repeat(np.eye(fine // 2, dtype=np.float32), 2, 0)


def shards(conserved, potential):
    cells_x, cells_y, cells_z = potential.shape
    count_x, count_y, count_z = (lax.axis_size(axis) for axis in AXES)
    devices = count_x * count_y * count_z
    lines = cells_x + 2 * WIDE
    block, whole, flat = (cells_x, cells_y, cells_z), conserved.shape, (5, cells_x * cells_y, cells_z)
    side, slab, ends = (2 * WIDE + 8, cells_y, cells_z), (2 * lines + 16, 8, cells_z), end_columns(cells_z, WIDE)
    fluid_rows = conserved.reshape(flat)

    head, tail = call(pack_x_kernel, [side] * 2, (), [block, whole])(potential, conserved)
    x_left, x_right = shift(tail, "gx", 1), shift(head, "gx", -1)
    head, tail = call(pack_y_kernel, [slab] * 2, (), [block, (1,) + block, flat, side, side])(
        potential, conserved, fluid_rows, x_left, x_right
    )
    y_left, y_right = shift(tail, "gy", 1), shift(head, "gy", -1)
    fluid, *sides, head, tail = lax.optimization_barrier((conserved, x_left, x_right, head, tail))
    update = call(flux_x_kernel, [whole], [(cells_x + 4, 5) + block[1:], (cells_x + 1, 5) + block[1:]])(fluid, *sides)[0]
    y_left, y_right, update = lax.optimization_barrier((y_left, y_right, update))
    columns = (8, 64 * lines + 4 * cells_x * cells_y)
    main, head, tail = call(
        pack_z_kernel,
        [(2 * lines, 32, cells_z), columns, columns],
        (),
        [block, (1,) + block, flat, side, side, slab, slab, ends.shape],
    )(potential, conserved, fluid_rows, x_left, x_right, y_left, y_right, ends)
    z_left, z_right = shift(tail, "gz", 1), shift(head, "gz", -1)
    fluid, *sides, update, head = lax.optimization_barrier((conserved, y_left, y_right, update, head))
    update = call(flux_y_kernel, [whole], [(4, 8 * cells_x, cells_z)])(fluid, *sides, update)[0]
    z_left, z_right, update = lax.optimization_barrier((z_left, z_right, update))

    pair_two = np.zeros((4, 128, 4, 32), np.float32)
    for part in range(4):
        pair_two[part, :64, part] = 0.125 * halved(64)
    window = (32, 32, 2 * cells_z)
    sizes = [window, window, (16, 16, 128), (8, 16, 128), (16, 8, 128), (8, 256), (8, 256), (devices * 5, 128)]
    tables = (0.125 * halved(256), pair_two.reshape(512, 128))
    values, source, one, one_x, one_y, one_head, one_tail, payload = call(
        pre_kernel,
        sizes,
        [window, window, (512, 256), (512, 128), (16, 16, 128), (64, 128)],
        late=2,
    )(main, z_left, z_right, ends, end_columns(64, 5), conserved, *tables)

    one_halo = [shift(one_x, "gx", 1), shift(one_x, "gx", -1), shift(one_y, "gy", 1), shift(one_y, "gy", -1)]
    one_halo.append(shift(one_tail, "gz", 1))
    gathered = lax.all_to_all(payload.reshape(devices, 1, 640), AXES, 0, 0, tiled=True).reshape(devices * 5, 128)

    fluid, update, *sides, _ = lax.optimization_barrier((conserved, update, z_left, z_right, payload))
    update = call(flux_z_kernel, [whole], [(32 * cells_x, cells_z), (64 * cells_x, cells_z)])(fluid, *sides, ends, update)[0]
    one_head, update = lax.optimization_barrier((one_head, update))
    one_halo.append(shift(one_head, "gz", -1))
    planes, groups = 4 * count_x, count_y
    position = jnp.stack([lax.axis_index(axis) for axis in AXES]).astype(jnp.int32)
    operands = (gathered, values, source, one, *one_halo, conserved, update)
    operands += coarse_tables(planes, groups, 64.0) + (pick_table(), place_columns(64, 5), halved(256).T)
    order = (12, 13, 14, 15, 16, 17, 3, 4, 5, 6, 7, 8, 9, 18, 19, 1, 2, 10, 11)
    tiles = planes * groups * 8
    updated, potential_out = pl.pallas_call(
        functools.partial(post_kernel, planes, groups, float(devices * cells_x * cells_y * cells_z)),
        out_shape=[jax.ShapeDtypeStruct(array.shape, jnp.float32) for array in (conserved, potential)],
        in_specs=[pl.BlockSpec(memory_space=pltpu.SMEM)]
        + [pl.BlockSpec(memory_space=pl.ANY if number else pltpu.VMEM) for number in range(len(operands))],
        scratch_shapes=[
            pltpu.VMEM(shape, jnp.float32)
            for shape in (
                (tiles + 8, 128), (tiles, 128), (tiles // 2, 128), (24, 384), (384, 128),
                (24, 24, 128), (24, 24, 128), (400, 128), (400, 128), (32, 32, 256),
            )
        ]
        + [pltpu.VMEM(operands[number].shape, jnp.float32) for number in order]
        + [pltpu.SemaphoreType.DMA((len(order),))],
        compiler_params=BIG,
    )(position, *operands)
    return (updated, potential_out)


def solution(mesh):
    in_specs = (P(None, "gx", "gy", "gz"), P("gx", "gy", "gz"))
    out_specs = (P(None, "gx", "gy", "gz"), P("gx", "gy", "gz"))
    return jax.shard_map(shards, mesh=mesh, in_specs=in_specs, out_specs=out_specs, check_vma=False)
```

```python
import functools

import numpy as np
import jax
import jax.numpy as jnp
from jax import lax
from jax.experimental import pallas as pl
from jax.experimental.pallas import tpu as pltpu
from jax.sharding import PartitionSpec as P

LEVELS = 3


gamma_gas = 5.0 / 3.0
courant = 0.4
coupling = 0.01


def primitives(density, first, second, third, energy):
    inverse = 1.0 / density
    kinetic = 0.5 * inverse * (first * first + second * second + third * third)
    pressure = (gamma_gas - 1.0) * (energy - kinetic)
    return [density, first * inverse, second * inverse, third * inverse, pressure]


def limited(first, second):
    return jnp.maximum(0.0, jnp.minimum(first, second)) + jnp.minimum(0.0, jnp.maximum(first, second))


def face_flux(before, centre, after_one, after_two, normal):
    lefts, rights = [], []
    for one, two, three, four in zip(before, centre, after_one, after_two):
        middle = three - two
        lefts.append(two + 0.5 * limited(two - one, middle))
        rights.append(three - 0.5 * limited(middle, four - three))
    along = 1 + normal
    others = [member for member in (1, 2, 3) if member != along]

    def unpack(state):
        density, speed, pressure = state[0], state[along], state[4]
        inverse = 1.0 / density
        squares = speed * speed + state[others[0]] * state[others[0]] + state[others[1]] * state[others[1]]
        energy = pressure * (1.0 / (gamma_gas - 1.0)) + 0.5 * density * squares
        return inverse, energy, jnp.sqrt(gamma_gas * pressure * inverse)

    left_inverse, left_energy, left_sound = unpack(lefts)
    right_inverse, right_energy, right_sound = unpack(rights)
    left_speed, right_speed = lefts[along], rights[along]
    low_wave = jnp.minimum(left_speed - left_sound, right_speed - right_sound)
    high_wave = jnp.maximum(left_speed + left_sound, right_speed + right_sound)
    left_mass = lefts[0] * (low_wave - left_speed)
    right_mass = rights[0] * (high_wave - right_speed)
    star_wave = (rights[4] - lefts[4] + left_mass * left_speed - right_mass * right_speed) / (left_mass - right_mass)
    from_left = jnp.logical_or(low_wave >= 0.0, star_wave >= 0.0)
    state = [jnp.where(from_left, one, two) for one, two in zip(lefts, rights)]
    inverse = jnp.where(from_left, left_inverse, right_inverse)
    energy = jnp.where(from_left, left_energy, right_energy)
    wave = jnp.where(from_left, low_wave, high_wave)
    rate = jnp.where(from_left, left_mass, right_mass)
    unstarred = jnp.where(from_left, -low_wave, high_wave) <= 0.0
    density, speed, pressure = state[0], state[along], state[4]
    carried = density * speed
    spread = 1.0 / (wave - star_wave)
    factor = rate * spread
    starred_energy = factor * (energy * inverse) + (star_wave - speed) * (factor * star_wave + pressure * spread)

    def jump(starred, stored):
        return jnp.where(unstarred, 0.0, wave * (starred - stored))

    mass_flux = carried + jump(factor, density)
    flux = [None] * 5
    flux[0] = mass_flux
    flux[along] = carried * speed + pressure + jump(factor * star_wave, carried)
    for member in others:
        flux[member] = state[member] * mass_flux
    flux[4] = speed * (energy + pressure) + jump(starred_energy, energy)
    return flux


AXES = ("gx", "gy", "gz")
EXACT = lax.Precision.HIGHEST
SIXTH = 1.0 / 6.0
SMALL = pltpu.CompilerParams(vmem_limit_bytes=20 * 1024 * 1024)
PRE = pltpu.CompilerParams(vmem_limit_bytes=60 * 1024 * 1024)
BIG = pltpu.CompilerParams(vmem_limit_bytes=56 * 1024 * 1024)


def shift(payload, axis, step):
    count = lax.axis_size(axis)
    return lax.ppermute(payload, axis, [(i, (i + step) % count) for i in range(count)])


def dot(left, right, dims=((1,), (0,))):
    return lax.dot_general(left, right, (dims, ((), ())), precision=EXACT, preferred_element_type=jnp.float32)


def turn(values, step, axis):
    return pltpu.roll(values, step % values.shape[axis], axis)


def plane_sum(cells):
    total_sum = turn(cells, -1, 0) + turn(cells, 1, 0)
    return total_sum + turn(cells, -1, 1) + turn(cells, 1, 1)


def parity_plane(shape):
    return (lax.broadcasted_iota(jnp.int32, shape, 0) + lax.broadcasted_iota(jnp.int32, shape, 1)) & 1


def slab_sum(ref, place):
    count = ref.shape[0]
    return ref[lax.rem(place + 1, count)] + ref[lax.rem(place + count - 1, count)] + plane_sum(ref[place])


def relax(ref, source_of, spacing_sq, colour, first, count):
    extent = ref.shape[0]
    plane = parity_plane(ref.shape[1:])

    def body(step, carry):
        places = [lax.rem(4 * step + part + (first % extent), extent) for part in range(4)]
        fresh = []
        for place in places:
            renewed = (slab_sum(ref, place) - spacing_sq * source_of(place)) * SIXTH
            fresh.append(jnp.where(plane == ((colour + place) & 1), renewed, ref[place]))
        for place, cells in zip(places, fresh):
            ref[place] = cells
        return carry

    lax.fori_loop(0, (count + 3) // 4, body, 0)


WIDE = 7


def end_columns(extent, width):
    table = np.zeros((16, 128), np.float32)
    table[np.arange(width), np.arange(width)] = 1.0
    table[8 + np.arange(width), extent - width + np.arange(width)] = 1.0
    return table


def place_columns(extent, width):
    table = np.zeros((16, 128), np.float32)
    table[np.arange(width), (extent + np.arange(width)) % 128] = 1.0
    table[8 + np.arange(width), 128 - width + np.arange(width)] = 1.0
    return table


def pack_x_kernel(phi, fluid, head, tail):
    extent = phi.shape[0]
    for start, flow_start, out in ((0, 0, head), (extent - WIDE, extent - 2, tail)):
        out[:WIDE] = phi[start : start + WIDE]
        out[WIDE : 2 * WIDE] = fluid[0, start : start + WIDE]
        for part in range(4):
            out[2 * WIDE + 2 * part : 2 * WIDE + 2 * part + 2] = fluid[1 + part, flow_start : flow_start + 2]


def pack_y_kernel(phi, fluid, flat, left, right, head, tail):
    extent = phi.shape[0]
    lines = extent + 2 * WIDE
    for number, own in ((0, phi), (1, fluid.at[0])):
        base = number * lines
        arrived = pl.ds(number * WIDE, WIDE)
        for rows, out in ((pl.ds(0, 8), head), (pl.ds(8, 8), tail)):
            out[pl.ds(base, extent)] = own[:, rows]
            out[pl.ds(base + extent, WIDE)] = right[arrived, rows]
            out[pl.ds(base + extent + WIDE, WIDE)] = left[arrived, rows]
    for start, out in ((0, head), (14, tail)):
        for part in range(4):
            for row in range(2):
                place = 2 * lines + 2 * (2 * part + row)
                cells = flat.at[1 + part][pl.ds(start + row, extent, stride=16), :]
                out[place : place + 2] = cells.reshape(2, 8, 128)


def pack_z_kernel(phi, fluid, flat, x_left, x_right, y_left, y_right, ends, main, head, tail):
    extent = phi.shape[0]
    lines = extent + 2 * WIDE
    for number, own in ((0, phi), (1, fluid.at[0])):
        base = number * lines
        arrived = pl.ds(number * WIDE, WIDE)
        main[pl.ds(base, extent), :16] = own[...]
        main[pl.ds(base + extent, WIDE), :16] = x_right[arrived]
        main[pl.ds(base + extent + WIDE, WIDE), :16] = x_left[arrived]
        main[pl.ds(base, lines), 16:24] = y_right[pl.ds(base, lines)]
        main[pl.ds(base, lines), 24:] = y_left[pl.ds(base, lines)]
    columns = dot(ends[...], main[...].reshape(2 * lines * 32, 128), ((1,), (1,)))
    head[:, : 64 * lines] = columns[:8]
    tail[:, : 64 * lines] = columns[8:]
    columns = dot(ends[...], flat[1:].reshape(4 * flat.shape[1], 128), ((1,), (1,)))
    head[:, 64 * lines :] = columns[:8]
    tail[:, 64 * lines :] = columns[8:]


def pre_kernel(
    main, z_left, z_right, ends, ends_one, conserved, pair_z, pair_two,
    values_out, source_out, one, one_x, one_y, one_head, one_tail, payload,
    values, source, sums, halves, swept, rows, leaving,
):
    lines = main.shape[0] // 2
    extent = lines - 2 * WIDE
    sides = jnp.concatenate([z_right[:, : 64 * lines], z_left[:, : 64 * lines]], 0)
    beside = dot(sides, ends[...], ((0,), (0,))).reshape(2 * lines, 32, 128)
    for number, ref, scale in ((0, values, None), (1, source, coupling)):
        base = number * lines
        gap = extent + WIDE
        ref[gap : 32 - WIDE] = jnp.zeros((32 - WIDE - gap, 32, 256), jnp.float32)
        for cells, columns in ((main, slice(0, 128)), (beside, slice(128, 256))):
            upper = cells[base : base + gap]
            lower = cells[base + gap : base + lines]
            ref[:gap, :, columns] = upper if scale is None else scale * upper
            ref[32 - WIDE :, :, columns] = lower if scale is None else scale * lower

    source_copy = pltpu.make_async_copy(source, source_out, leaving.at[0])
    source_copy.start()
    relax(values, lambda place: source[place], 1.0, 0, -6, extent + 12)
    relax(values, lambda place: source[place], 1.0, 1, -5, extent + 10)
    values_copy = pltpu.make_async_copy(values, values_out, leaving.at[1])
    values_copy.start()

    sums[10 * 32 : 14 * 32, :] = jnp.zeros((4 * 32, 256), jnp.float32)

    def defect_pair(turned, carry):
        step = lax.rem(turned + 14, 16)
        total_sum = jnp.zeros((32, 256), jnp.float32)
        for part in range(2):
            place = 2 * step + part
            total_sum += source[place] - (slab_sum(values, place) - 6.0 * values[place])
        sums[pl.ds(pl.multiple_of(step * 32, 32), 32), :] = total_sum
        return carry

    lax.fori_loop(0, 12, defect_pair, 0, unroll=2)
    halves[...] = dot(sums[...], pair_z[...])
    one[...] = (halves[pl.ds(0, 256, stride=2), :] + halves[pl.ds(1, 256, stride=2), :]).reshape(16, 16, 128)
    one_x[...] = one[:8]
    one_y[...] = one[:, :8]
    columns = dot(ends_one[...], one[...].reshape(256, 128), ((1,), (1,)))
    one_head[...] = columns[:8]
    one_tail[...] = columns[8:]

    plane = parity_plane((16, 128))
    for place in range(16):
        swept[place] = jnp.where(plane == (place & 1), one[place] * (-4.0 * SIXTH), 0.0)
    relax(swept, lambda place: one[place], 4.0, 1, 0, 16)
    for step in range(8):
        total_sum = jnp.zeros((16, 128), jnp.float32)
        for part in range(2):
            place = 2 * step + part
            total_sum += one[place] - (slab_sum(swept, place) - 6.0 * swept[place]) * 0.25
        rows[8 * step : 8 * step + 8, :] = total_sum[:8]
    packed = jnp.zeros((8, 128), jnp.float32)
    for part in range(4):
        both = rows[pl.ds(2 * part, 8, stride=8), :] + rows[pl.ds(2 * part + 1, 8, stride=8), :]
        packed += dot(both, pair_two[128 * part : 128 * part + 128, :])

    def measure_slab(place, carry):
        mass, speed = carry
        density = conserved[0, place]
        inverse = 1.0 / density
        first, second, third = conserved[1, place], conserved[2, place], conserved[3, place]
        kinetic = 0.5 * inverse * (first * first + second * second + third * third)
        pressure = (gamma_gas - 1.0) * (conserved[4, place] - kinetic)
        signal = (jnp.abs(first) + jnp.abs(second) + jnp.abs(third)) * inverse
        signal += 3.0 * jnp.sqrt(gamma_gas * pressure * inverse)
        return mass + density, jnp.maximum(speed, signal)

    blank = jnp.zeros((16, 128), jnp.float32)
    mass, speed = lax.fori_loop(0, extent, measure_slab, (blank, blank), unroll=2)
    mass = jnp.sum(jnp.sum(mass, axis=0, keepdims=True), axis=1, keepdims=True)
    speed = jnp.max(jnp.max(speed, axis=0, keepdims=True), axis=1, keepdims=True)
    lane = lax.broadcasted_iota(jnp.int32, (1, 128), 1)
    extra = jnp.where(lane == 0, mass, jnp.where(lane == 1, speed, 0.0))
    count = payload.shape[0] // 5
    for part in range(4):
        payload[pl.ds(part, count, stride=5), :] = jnp.broadcast_to(packed[part : part + 1], (count, 128))
    payload[pl.ds(4, count, stride=5), :] = jnp.broadcast_to(extra, (count, 128))
    source_copy.wait()
    values_copy.wait()


def cas(extent):
    angle = 2.0 * np.pi / extent * np.outer(np.arange(extent), np.arange(extent))
    return (np.cos(angle) + np.sin(angle)) / np.sqrt(extent)


def eigen(extent, spacing_sq):
    return (2.0 * np.cos(2.0 * np.pi / extent * np.arange(extent)) - 2.0) / spacing_sq


def coarse_tables(planes, groups, spacing_sq):
    half = planes // 2
    line = cas(128)
    same = np.repeat(np.eye(2), 2, 0)
    spread = np.repeat(line, 2, 0).reshape(8, 32, 128)
    forward = np.einsum("ab,gzk->gazbk", same, spread).reshape(1024, 256)
    across = cas(2 * groups).reshape(2 * groups, groups, 2)
    plane = np.einsum("px,qgb->pqbxg", cas(half), across).reshape(2 * groups * half, 2 * groups * half)
    total = (eigen(half, spacing_sq)[:, None] + eigen(2 * groups, spacing_sq)).reshape(-1, 1) + eigen(128, spacing_sq)
    total[0, 0] = 1.0
    inverse = 1.0 / total
    inverse[0, 0] = 0.0
    tables = (0.125 * forward, plane, inverse, plane.T, forward.T)
    return tuple(np.ascontiguousarray(table, dtype=np.float32) for table in tables)


def pick_table():
    table = np.zeros((3, 4, 32, 4, 128), np.float32)
    for line in range(4):
        for cell in range(32):
            table[0, line, cell, line, 2 * cell : 2 * cell + 2] = 1.0
        for cell in range(2):
            table[1, line, cell, line, 64 + 2 * cell : 66 + 2 * cell] = 1.0
            table[2, line, 30 + cell, line, 124 + 2 * cell : 126 + 2 * cell] = 1.0
    return table.reshape(384, 512)


def post_kernel(
    planes, groups, cells_total,
    where_ref, gathered, values, source, one_own, x_left, x_right, y_left, y_right, z_left, z_right, conserved, update,
    to_line, to_plane, inverse, from_plane, from_line, pick, place_one, refine_z,
    updated, potential_out,
    coarse, rhs, stage, chosen, extra, one_rhs, one, fine_low, fine_high, work,
    *held,
):
    far = (to_line, to_plane, inverse, from_plane, from_line, pick, one_own, x_left, x_right, y_left, y_right, z_left, z_right)
    far += (place_one, refine_z, values, source, conserved, update)
    arrivals = held[-1]
    copies = [pltpu.make_async_copy(ref, near, arrivals.at[number]) for number, (ref, near) in enumerate(zip(far, held))]
    for copy in copies:
        copy.start()
    to_line, to_plane, inverse, from_plane, from_line, pick, one_own, x_left, x_right, y_left, y_right, z_left, z_right = held[:13]
    place_one, refine_z, values, source, conserved, update = held[13:-1]

    last = gathered[pl.ds(4, gathered.shape[0] // 5, stride=5), :]
    lane_row = lax.broadcasted_iota(jnp.int32, (1, 128), 1)
    mass = jnp.sum(jnp.where(lane_row == 0, jnp.sum(last, axis=0, keepdims=True), 0.0), axis=1, keepdims=True)
    speed = jnp.sum(jnp.where(lane_row == 1, jnp.max(last, axis=0, keepdims=True), 0.0), axis=1, keepdims=True)
    offset = mass * (-coupling / cells_total)
    step_size = courant / speed

    spacing_sq = 16.0
    lane = lax.broadcasted_iota(jnp.int32, (8, 128), 1)
    cell = lane & 31
    plane = (cell + (lane >> 5)) & 1

    def tile(place, group):
        return pl.ds(pl.multiple_of((place * groups + group) * 8, 8), 8)

    def tile_sum(place, group):
        centre = coarse[tile(place, group), :]
        total_sum = coarse[tile(lax.rem(place + 1, planes), group), :]
        total_sum += coarse[tile(lax.rem(place + planes - 1, planes), group), :]
        after = coarse[tile(place, (group + 1) % groups), :]
        before = coarse[tile(place, (group + groups - 1) % groups), :]
        total_sum += turn(jnp.where(lane < 32, after, centre), -32, 1)
        total_sum += turn(jnp.where(lane >= 96, before, centre), 32, 1)
        total_sum += jnp.where(cell == 31, turn(turn(centre, -1, 0), 31, 1), turn(centre, -1, 1))
        total_sum += jnp.where(cell == 0, turn(turn(centre, 1, 0), -31, 1), turn(centre, 1, 1))
        return centre, total_sum

    def coarse_relax(colour):
        def body(step, carry):
            tiles = [(4 * step + part, group) for part in range(4) for group in range(groups)]
            fresh = []
            for place, group in tiles:
                centre, total_sum = tile_sum(place, group)
                renewed = (total_sum - spacing_sq * rhs[tile(place, group), :]) * SIXTH
                fresh.append(jnp.where(plane == ((colour + place) & 1), renewed, centre))
            for (place, group), cells in zip(tiles, fresh):
                coarse[tile(place, group), :] = cells
            return carry

        lax.fori_loop(0, planes // 4, body, 0)

    for place in range(planes):
        for group in range(groups):
            first_row = ((place // 4) * groups + group) * 8
            cells = gathered[pl.ds(5 * first_row + place % 4, 8, stride=5), :] + offset
            here = pl.ds((place * groups + group) * 8, 8)
            rhs[here, :] = cells
            coarse[here, :] = jnp.where(plane == (place & 1), cells * (-spacing_sq * SIXTH), 0.0)
    coarse_relax(1)

    def defect_pair(step, carry):
        for group in range(groups):
            total = jnp.zeros((8, 128), jnp.float32)
            for part in range(2):
                place = 2 * step + part
                centre, total_sum = tile_sum(place, group)
                total += rhs[tile(place, group), :] - (total_sum - 6.0 * centre) * (1.0 / spacing_sq)
            stage[tile(step, group), :] = total
        return carry

    half = planes // 2
    lines = half * groups
    for copy in copies[:5]:
        copy.wait()
    lax.fori_loop(0, half, defect_pair, 0, unroll=2)
    modes = jnp.zeros((lines, 256), jnp.float32)
    for part in range(8):
        modes += dot(stage[pl.ds(part, lines, stride=8), :], to_line[128 * part : 128 * part + 128, :])
    modes = jnp.concatenate([modes[:, :128], modes[:, 128:]], 0)
    modes = dot(from_plane[...], dot(to_plane[...], modes) * inverse[...])
    modes = jnp.concatenate([modes[:lines], modes[lines:]], 1)
    for part in range(8):
        stage[pl.ds(part, lines, stride=8), :] = dot(modes, from_line[:, 128 * part : 128 * part + 128])

    def add_back(step, carry):
        for group in range(groups):
            correction = stage[tile(step, group), :]
            for part in range(2):
                coarse[tile(2 * step + part, group), :] += correction
        return carry

    lax.fori_loop(0, half, add_back, 0, unroll=2)
    coarse_relax(0)
    coarse_relax(1)

    my_x, my_y, my_z = where_ref[0], where_ref[1], where_ref[2]
    for number, along_y in enumerate((0, 1, groups - 1)):
        for row, along_x in enumerate((0, 1, 2, 3, 4, 5, planes - 2, planes - 1)):
            for column, along_z in enumerate((0, 1, 7)):
                place = lax.rem(4 * my_x + along_x, planes)
                group = lax.rem(my_y + along_y, groups)
                line = lax.rem(my_z + along_z, 8)
                chosen[8 * number + row : 8 * number + row + 1, 128 * column : 128 * column + 128] = coarse[
                    pl.ds((place * groups + group) * 8 + line, 1), :
                ]
    for copy in copies[5:15]:
        copy.wait()
    picked = dot(chosen[...], pick[...])
    for number, line, slot in ((0, 0, 0), (0, 1, 2), (0, 2, 4), (0, 3, 6), (1, 0, 8), (1, 1, 10), (2, 2, 20), (2, 3, 22)):
        rows = picked[8 * number : 8 * number + 8, 128 * line : 128 * line + 128]
        for part in range(2):
            for twice in range(2):
                extra[pl.ds(24 * part + slot + twice, 8, stride=48), :] = rows

    sides = jnp.concatenate([z_right[...], z_left[...]], 0)
    beside = dot(sides, place_one[...], ((0,), (0,))).reshape(16, 16, 128)
    line_one = lax.broadcasted_iota(jnp.int32, (24, 128), 0)
    lane_one = lax.broadcasted_iota(jnp.int32, (24, 128), 1)
    plane_one = (line_one + lane_one) & 1
    from_z = jnp.logical_and(lane_one >= 64, jnp.logical_or(line_one < 10, line_one >= 22))
    for place in range(24):
        if place < 10 or place >= 22:
            row = place if place < 10 else place - 8
            cells = jnp.concatenate([one_own[row, :8], y_right[row], y_left[row]], 0)
            sideways = beside[row]
            cells = jnp.where(from_z, jnp.concatenate([sideways, sideways[8:]], 0), cells)
        elif place < 13 or place >= 19:
            cells = x_right[place - 8] if place < 13 else x_left[place - 16]
            cells = jnp.concatenate([cells, cells[8:]], 0)
        else:
            cells = jnp.zeros((24, 128), jnp.float32)
        cells = cells + offset
        one_rhs[place] = cells
        one[place] = jnp.where(plane_one == (place & 1), cells * (-4.0 * SIXTH), 0.0)
    relax(one, lambda place: one_rhs[place], 4.0, 1, -4, 16)
    for row in range(16):
        place = row if row < 12 else row + 8
        one[place] += extra[24 * row : 24 * row + 24, :]
    relax(one, lambda place: one_rhs[place], 4.0, 0, -3, 14)
    relax(one, lambda place: one_rhs[place], 4.0, 1, -2, 12)

    wide = jnp.concatenate([one[0:10], one[22:24]], 0).reshape(288, 128)
    wide = dot(wide, refine_z[...])
    for row in range(12):
        for part, fine in ((0, fine_low), (1, fine_high)):
            cells = wide[24 * row : 24 * row + 24, 128 * part : 128 * part + 128]
            for twice in range(2):
                fine[pl.ds(32 * row + twice, 8, stride=2), :] = cells[:8]
                fine[pl.ds(32 * row + 16 + twice, 4, stride=2), :] = cells[8:12]
                fine[pl.ds(32 * row + 24 + twice, 4, stride=2), :] = cells[20:24]
    plane_fine = parity_plane((32, 256))
    for copy in copies[15:]:
        copy.wait()
    for place in tuple(range(20)) + tuple(range(28, 32)):
        row = place // 2 if place < 20 else place // 2 - 4
        lift = jnp.concatenate([fine_low[32 * row : 32 * row + 32, :], fine_high[32 * row : 32 * row + 32, :]], 1)
        moved = jnp.where(plane_fine == (place & 1), offset * (-SIXTH), offset * (-2.0 * SIXTH))
        work[place] = values[place] + (lift + moved)
    extent = potential_out.shape[0]
    relax(work, lambda place: source[place] + offset, 1.0, 0, -2, extent + 4)
    relax(work, lambda place: source[place] + offset, 1.0, 1, -1, extent + 2)

    def finish(place, carry):
        cells = work[place]
        after, before = work[lax.rem(place + 1, 32)], work[lax.rem(place + 31, 32)]
        along_x = (after[:16, :128] - before[:16, :128]) * 0.5
        along_y = ((turn(cells, -1, 0) - turn(cells, 1, 0)) * 0.5)[:16, :128]
        along_z = ((turn(cells, -1, 1) - turn(cells, 1, 1)) * 0.5)[:16, :128]
        potential_out[place] = cells[:16, :128]
        density = conserved[0, place]
        first, second, third = conserved[1, place], conserved[2, place], conserved[3, place]
        energy_source = first * along_x + second * along_y + third * along_z
        updated[0, place] = density + step_size * update[0, place]
        updated[1, place] = first + step_size * (update[1, place] - density * along_x)
        updated[2, place] = second + step_size * (update[2, place] - density * along_y)
        updated[3, place] = third + step_size * (update[3, place] - density * along_z)
        updated[4, place] = conserved[4, place] + step_size * (update[4, place] - energy_source)
        return carry

    lax.fori_loop(0, extent, finish, 0, unroll=2)


def flux_x_kernel(fluid, left, right, out, states, fluxes):
    extent = fluid.shape[1]

    def fill(place, cells):
        for member, values in enumerate(primitives(*cells)):
            states[place, member] = values

    for row in range(2):
        for place, arrived, at in ((row, left, 2 * WIDE - 2 + row), (extent + 2 + row, right, WIDE + row)):
            fill(place, [arrived[at]] + [arrived[2 * WIDE + 2 * part + row] for part in range(4)])

    def own(place, carry):
        fill(place + 2, [fluid[member, place] for member in range(5)])
        return carry

    def face(place, carry):
        around = [[states[place + step, member] for member in range(5)] for step in range(4)]
        for member, values in enumerate(face_flux(*around, 0)):
            fluxes[place, member] = values
        return carry

    def difference(place, carry):
        for member in range(5):
            out[member, place] = fluxes[place, member] - fluxes[place + 1, member]
        return carry

    lax.fori_loop(0, extent, own, 0, unroll=2)
    lax.fori_loop(0, extent + 1, face, 0)
    lax.fori_loop(0, extent, difference, 0)


def flux_y_kernel(fluid, left, right, part, out, beside):
    extent = fluid.shape[1]
    lines = extent + 2 * WIDE
    row = lax.broadcasted_iota(jnp.int32, (8, 128), 0)
    for member in range(4):
        for line in range(2):
            place = 2 * lines + 2 * (2 * member + line)
            beside.at[member][pl.ds(line, extent, stride=8), :] = right[place : place + 2].reshape(16, 128)
            beside.at[member][pl.ds(6 + line, extent, stride=8), :] = left[place : place + 2].reshape(16, 128)

    def slab(place, carry):
        far = jnp.where(row < 4, right[lines + place], left[lines + place])
        cells = [jnp.concatenate([fluid[0, place], far], 0)]
        for member in range(4):
            far = beside[member, pl.ds(pl.multiple_of(8 * place, 8), 8), :]
            cells.append(jnp.concatenate([fluid[1 + member, place], far], 0))
        state = primitives(*cells)
        around = [[turn(values, -step, 0) for values in state] for step in (-1, 0, 1, 2)]
        for member, values in enumerate(face_flux(around[0], state, around[2], around[3], 1)):
            out[member, place] = part[member, place] + (turn(values, 1, 0) - values)[:16]
        return carry

    lax.fori_loop(0, extent, slab, 0)


def flux_z_kernel(fluid, left, right, ends, part, out, thin, beside):
    extent = fluid.shape[1]
    lines = extent + 2 * WIDE
    for start, count, ref in ((32 * lines, 32 * extent, thin), (64 * lines, 64 * extent, beside)):
        sides = jnp.concatenate([right[:, start : start + count], left[:, start : start + count]], 0)
        ref[...] = dot(sides, ends[...], ((0,), (0,)))

    def slab(place, carry):
        far = thin[pl.ds(pl.multiple_of(32 * place, 32), 16), :]
        cells = [jnp.concatenate([fluid[0, place], far], 1)]
        for member in range(4):
            far = beside[pl.ds(pl.multiple_of(16 * extent * member + 16 * place, 16), 16), :]
            cells.append(jnp.concatenate([fluid[1 + member, place], far], 1))
        state = primitives(*cells)
        around = [[turn(values, -step, 1) for values in state] for step in (-1, 0, 1, 2)]
        for member, values in enumerate(face_flux(around[0], state, around[2], around[3], 2)):
            out[member, place] = part[member, place] + (turn(values, 1, 1) - values)[:, :128]
        return carry

    lax.fori_loop(0, extent, slab, 0)


def call(kernel, shapes, scratch=(), operands=None, late=0):
    extra = {}
    if late:
        results = [pl.BlockSpec(memory_space=pl.ANY if number < late else pltpu.VMEM) for number in range(len(shapes))]
        extra = dict(out_specs=results)
    if operands is not None:
        specs = [pl.BlockSpec(shape, functools.partial(lambda rank, step: (0,) * rank, len(shape))) for shape in operands]
        results = [pl.BlockSpec(shape, functools.partial(lambda rank, step: (0,) * rank, len(shape))) for shape in shapes]
        extra = dict(grid=(1,), in_specs=specs, out_specs=results)
    return pl.pallas_call(
        kernel,
        **extra,
        out_shape=[jax.ShapeDtypeStruct(shape, jnp.float32) for shape in shapes],
        scratch_shapes=[pltpu.VMEM(shape, jnp.float32) for shape in scratch]
        + ([pltpu.SemaphoreType.DMA((late,))] if late else []),
        compiler_params=PRE if late else SMALL,
    )


def halved(fine):
    return np.repeat(np.eye(fine // 2, dtype=np.float32), 2, 0)


def shards(conserved, potential):
    cells_x, cells_y, cells_z = potential.shape
    count_x, count_y, count_z = (lax.axis_size(axis) for axis in AXES)
    devices = count_x * count_y * count_z
    lines = cells_x + 2 * WIDE
    block, whole, flat = (cells_x, cells_y, cells_z), conserved.shape, (5, cells_x * cells_y, cells_z)
    side, slab, ends = (2 * WIDE + 8, cells_y, cells_z), (2 * lines + 16, 8, cells_z), end_columns(cells_z, WIDE)
    fluid_rows = conserved.reshape(flat)

    head, tail = call(pack_x_kernel, [side] * 2, (), [block, whole])(potential, conserved)
    x_left, x_right = shift(tail, "gx", 1), shift(head, "gx", -1)
    head, tail = call(pack_y_kernel, [slab] * 2, (), [block, (1,) + block, flat, side, side])(
        potential, conserved, fluid_rows, x_left, x_right
    )
    y_left, y_right = shift(tail, "gy", 1), shift(head, "gy", -1)
    fluid, *sides, head, tail = lax.optimization_barrier((conserved, x_left, x_right, head, tail))
    update = call(flux_x_kernel, [whole], [(cells_x + 4, 5) + block[1:], (cells_x + 1, 5) + block[1:]])(fluid, *sides)[0]
    y_left, y_right, update = lax.optimization_barrier((y_left, y_right, update))
    columns = (8, 64 * lines + 4 * cells_x * cells_y)
    main, head, tail = call(
        pack_z_kernel,
        [(2 * lines, 32, cells_z), columns, columns],
        (),
        [block, (1,) + block, flat, side, side, slab, slab, ends.shape],
    )(potential, conserved, fluid_rows, x_left, x_right, y_left, y_right, ends)
    z_left, z_right = shift(tail, "gz", 1), shift(head, "gz", -1)
    fluid, *sides, update, head = lax.optimization_barrier((conserved, y_left, y_right, update, head))
    update = call(flux_y_kernel, [whole], [(4, 8 * cells_x, cells_z)])(fluid, *sides, update)[0]
    z_left, z_right, update = lax.optimization_barrier((z_left, z_right, update))

    pair_two = np.zeros((4, 128, 4, 32), np.float32)
    for part in range(4):
        pair_two[part, :64, part] = 0.125 * halved(64)
    window = (32, 32, 2 * cells_z)
    sizes = [window, window, (16, 16, 128), (8, 16, 128), (16, 8, 128), (8, 256), (8, 256), (devices * 5, 128)]
    tables = (0.125 * halved(256), pair_two.reshape(512, 128))
    values, source, one, one_x, one_y, one_head, one_tail, payload = call(
        pre_kernel,
        sizes,
        [window, window, (512, 256), (512, 128), (16, 16, 128), (64, 128)],
        late=2,
    )(main, z_left, z_right, ends, end_columns(64, 5), conserved, *tables)

    one_halo = [shift(one_x, "gx", 1), shift(one_x, "gx", -1), shift(one_y, "gy", 1), shift(one_y, "gy", -1)]
    one_halo.append(shift(one_tail, "gz", 1))
    gathered = lax.all_to_all(payload.reshape(devices, 1, 640), AXES, 0, 0, tiled=True).reshape(devices * 5, 128)

    fluid, update, *sides, _ = lax.optimization_barrier((conserved, update, z_left, z_right, payload))
    update = call(flux_z_kernel, [whole], [(32 * cells_x, cells_z), (64 * cells_x, cells_z)])(fluid, *sides, ends, update)[0]
    one_head, update = lax.optimization_barrier((one_head, update))
    one_halo.append(shift(one_head, "gz", -1))
    planes, groups = 4 * count_x, count_y
    position = jnp.stack([lax.axis_index(axis) for axis in AXES]).astype(jnp.int32)
    operands = (gathered, values, source, one, *one_halo, conserved, update)
    operands += coarse_tables(planes, groups, 64.0) + (pick_table(), place_columns(64, 5), halved(256).T)
    order = (12, 13, 14, 15, 16, 17, 3, 4, 5, 6, 7, 8, 9, 18, 19, 1, 2, 10, 11)
    tiles = planes * groups * 8
    updated, potential_out = pl.pallas_call(
        functools.partial(post_kernel, planes, groups, float(devices * cells_x * cells_y * cells_z)),
        out_shape=[jax.ShapeDtypeStruct(array.shape, jnp.float32) for array in (conserved, potential)],
        in_specs=[pl.BlockSpec(memory_space=pltpu.SMEM)]
        + [pl.BlockSpec(memory_space=pl.ANY if number else pltpu.VMEM) for number in range(len(operands))],
        scratch_shapes=[
            pltpu.VMEM(shape, jnp.float32)
            for shape in (
                (tiles + 8, 128), (tiles, 128), (tiles // 2, 128), (24, 384), (384, 128),
                (24, 24, 128), (24, 24, 128), (400, 128), (400, 128), (32, 32, 256),
            )
        ]
        + [pltpu.VMEM(operands[number].shape, jnp.float32) for number in order]
        + [pltpu.SemaphoreType.DMA((len(order),))],
        compiler_params=BIG,
    )(position, *operands)
    return (updated, potential_out)


def solution(mesh):
    in_specs = (P(None, "gx", "gy", "gz"), P("gx", "gy", "gz"))
    out_specs = (P(None, "gx", "gy", "gz"), P("gx", "gy", "gz"))
    return jax.shard_map(shards, mesh=mesh, in_specs=in_specs, out_specs=out_specs, check_vma=False)
```

```python
import functools

import numpy as np
import jax
import jax.numpy as jnp
from jax import lax
from jax.experimental import pallas as pl
from jax.experimental.pallas import tpu as pltpu
from jax.sharding import PartitionSpec as P

LEVELS = 3


gamma_gas = 5.0 / 3.0
courant = 0.4
coupling = 0.01


def primitives(density, first, second, third, energy):
    inverse = 1.0 / density
    kinetic = 0.5 * inverse * (first * first + second * second + third * third)
    pressure = (gamma_gas - 1.0) * (energy - kinetic)
    return [density, first * inverse, second * inverse, third * inverse, pressure]


def limited(first, second):
    return jnp.maximum(0.0, jnp.minimum(first, second)) + jnp.minimum(0.0, jnp.maximum(first, second))


def face_flux(before, centre, after_one, after_two, normal):
    lefts, rights = [], []
    for one, two, three, four in zip(before, centre, after_one, after_two):
        middle = three - two
        lefts.append(two + 0.5 * limited(two - one, middle))
        rights.append(three - 0.5 * limited(middle, four - three))
    along = 1 + normal
    others = [member for member in (1, 2, 3) if member != along]

    def unpack(state):
        density, speed, pressure = state[0], state[along], state[4]
        inverse = 1.0 / density
        squares = speed * speed + state[others[0]] * state[others[0]] + state[others[1]] * state[others[1]]
        energy = pressure * (1.0 / (gamma_gas - 1.0)) + 0.5 * density * squares
        return inverse, energy, jnp.sqrt(gamma_gas * pressure * inverse)

    left_inverse, left_energy, left_sound = unpack(lefts)
    right_inverse, right_energy, right_sound = unpack(rights)
    left_speed, right_speed = lefts[along], rights[along]
    low_wave = jnp.minimum(left_speed - left_sound, right_speed - right_sound)
    high_wave = jnp.maximum(left_speed + left_sound, right_speed + right_sound)
    left_mass = lefts[0] * (low_wave - left_speed)
    right_mass = rights[0] * (high_wave - right_speed)
    star_wave = (rights[4] - lefts[4] + left_mass * left_speed - right_mass * right_speed) / (left_mass - right_mass)
    from_left = jnp.logical_or(low_wave >= 0.0, star_wave >= 0.0)
    state = [jnp.where(from_left, one, two) for one, two in zip(lefts, rights)]
    inverse = jnp.where(from_left, left_inverse, right_inverse)
    energy = jnp.where(from_left, left_energy, right_energy)
    wave = jnp.where(from_left, low_wave, high_wave)
    rate = jnp.where(from_left, left_mass, right_mass)
    unstarred = jnp.where(from_left, -low_wave, high_wave) <= 0.0
    density, speed, pressure = state[0], state[along], state[4]
    carried = density * speed
    spread = 1.0 / (wave - star_wave)
    factor = rate * spread
    starred_energy = factor * (energy * inverse) + (star_wave - speed) * (factor * star_wave + pressure * spread)

    def jump(starred, stored):
        return jnp.where(unstarred, 0.0, wave * (starred - stored))

    mass_flux = carried + jump(factor, density)
    flux = [None] * 5
    flux[0] = mass_flux
    flux[along] = carried * speed + pressure + jump(factor * star_wave, carried)
    for member in others:
        flux[member] = state[member] * mass_flux
    flux[4] = speed * (energy + pressure) + jump(starred_energy, energy)
    return flux


AXES = ("gx", "gy", "gz")
EXACT = lax.Precision.HIGHEST
SIXTH = 1.0 / 6.0
SMALL = pltpu.CompilerParams(vmem_limit_bytes=20 * 1024 * 1024)
PRE = pltpu.CompilerParams(vmem_limit_bytes=60 * 1024 * 1024)
BIG = pltpu.CompilerParams(vmem_limit_bytes=56 * 1024 * 1024)


def shift(payload, axis, step):
    count = lax.axis_size(axis)
    return lax.ppermute(payload, axis, [(i, (i + step) % count) for i in range(count)])


def dot(left, right, dims=((1,), (0,))):
    return lax.dot_general(left, right, (dims, ((), ())), precision=EXACT, preferred_element_type=jnp.float32)


def turn(values, step, axis):
    return pltpu.roll(values, step % values.shape[axis], axis)


def plane_sum(cells):
    total_sum = turn(cells, -1, 0) + turn(cells, 1, 0)
    return total_sum + turn(cells, -1, 1) + turn(cells, 1, 1)


def parity_plane(shape):
    return (lax.broadcasted_iota(jnp.int32, shape, 0) + lax.broadcasted_iota(jnp.int32, shape, 1)) & 1


def slab_sum(ref, place):
    count = ref.shape[0]
    return ref[lax.rem(place + 1, count)] + ref[lax.rem(place + count - 1, count)] + plane_sum(ref[place])


def relax(ref, source_of, spacing_sq, colour, first, count):
    extent = ref.shape[0]
    plane = parity_plane(ref.shape[1:])
    batch = 4 if ref.shape[2] > 128 else 8

    def body(step, carry):
        places = [lax.rem(batch * step + part + (first % extent), extent) for part in range(batch)]
        fresh = []
        for place in places:
            renewed = (slab_sum(ref, place) - spacing_sq * source_of(place)) * SIXTH
            fresh.append(jnp.where(plane == ((colour + place) & 1), renewed, ref[place]))
        for place, cells in zip(places, fresh):
            ref[place] = cells
        return carry

    lax.fori_loop(0, (count + batch - 1) // batch, body, 0)


WIDE = 7


def end_columns(extent, width):
    table = np.zeros((16, 128), np.float32)
    table[np.arange(width), np.arange(width)] = 1.0
    table[8 + np.arange(width), extent - width + np.arange(width)] = 1.0
    return table


def place_columns(extent, width):
    table = np.zeros((16, 128), np.float32)
    table[np.arange(width), (extent + np.arange(width)) % 128] = 1.0
    table[8 + np.arange(width), 128 - width + np.arange(width)] = 1.0
    return table


def pack_x_kernel(phi, fluid, head, tail):
    extent = phi.shape[0]
    for start, flow_start, out in ((0, 0, head), (extent - WIDE, extent - 2, tail)):
        out[:WIDE] = phi[start : start + WIDE]
        out[WIDE : 2 * WIDE] = fluid[0, start : start + WIDE]
        for part in range(4):
            out[2 * WIDE + 2 * part : 2 * WIDE + 2 * part + 2] = fluid[1 + part, flow_start : flow_start + 2]


def pack_y_kernel(phi, fluid, flat, left, right, head, tail):
    extent = phi.shape[0]
    lines = extent + 2 * WIDE
    for number, own in ((0, phi), (1, fluid.at[0])):
        base = number * lines
        arrived = pl.ds(number * WIDE, WIDE)
        for rows, out in ((pl.ds(0, 8), head), (pl.ds(8, 8), tail)):
            out[pl.ds(base, extent)] = own[:, rows]
            out[pl.ds(base + extent, WIDE)] = right[arrived, rows]
            out[pl.ds(base + extent + WIDE, WIDE)] = left[arrived, rows]
    for start, out in ((0, head), (14, tail)):
        for part in range(4):
            for row in range(2):
                place = 2 * lines + 2 * (2 * part + row)
                cells = flat.at[1 + part][pl.ds(start + row, extent, stride=16), :]
                out[place : place + 2] = cells.reshape(2, 8, 128)


def pack_z_kernel(phi, fluid, flat, x_left, x_right, y_left, y_right, ends, main, head, tail):
    extent = phi.shape[0]
    lines = extent + 2 * WIDE
    for number, own in ((0, phi), (1, fluid.at[0])):
        base = number * lines
        arrived = pl.ds(number * WIDE, WIDE)
        main[pl.ds(base, extent), :16] = own[...]
        main[pl.ds(base + extent, WIDE), :16] = x_right[arrived]
        main[pl.ds(base + extent + WIDE, WIDE), :16] = x_left[arrived]
        main[pl.ds(base, lines), 16:24] = y_right[pl.ds(base, lines)]
        main[pl.ds(base, lines), 24:] = y_left[pl.ds(base, lines)]
    columns = dot(ends[...], main[...].reshape(2 * lines * 32, 128), ((1,), (1,)))
    head[:, : 64 * lines] = columns[:8]
    tail[:, : 64 * lines] = columns[8:]
    columns = dot(ends[...], flat[1:].reshape(4 * flat.shape[1], 128), ((1,), (1,)))
    head[:, 64 * lines :] = columns[:8]
    tail[:, 64 * lines :] = columns[8:]


def pre_kernel(
    main, z_left, z_right, ends, ends_one, conserved, pair_z, pair_two,
    values_out, source_out, one, one_x, one_y, one_head, one_tail, payload,
    values, source, sums, halves, swept, rows, leaving,
):
    lines = main.shape[0] // 2
    extent = lines - 2 * WIDE
    sides = jnp.concatenate([z_right[:, : 64 * lines], z_left[:, : 64 * lines]], 0)
    beside = dot(sides, ends[...], ((0,), (0,))).reshape(2 * lines, 32, 128)
    for number, ref, scale in ((0, values, None), (1, source, coupling)):
        base = number * lines
        gap = extent + WIDE
        ref[gap : 32 - WIDE] = jnp.zeros((32 - WIDE - gap, 32, 256), jnp.float32)
        for cells, columns in ((main, slice(0, 128)), (beside, slice(128, 256))):
            upper = cells[base : base + gap]
            lower = cells[base + gap : base + lines]
            ref[:gap, :, columns] = upper if scale is None else scale * upper
            ref[32 - WIDE :, :, columns] = lower if scale is None else scale * lower

    source_copy = pltpu.make_async_copy(source, source_out, leaving.at[0])
    source_copy.start()
    relax(values, lambda place: source[place], 1.0, 0, -6, extent + 12)
    relax(values, lambda place: source[place], 1.0, 1, -5, extent + 10)
    values_copy = pltpu.make_async_copy(values, values_out, leaving.at[1])
    values_copy.start()

    sums[10 * 32 : 14 * 32, :] = jnp.zeros((4 * 32, 256), jnp.float32)

    def defect_pair(turned, carry):
        step = lax.rem(turned + 14, 16)
        total_sum = jnp.zeros((32, 256), jnp.float32)
        for part in range(2):
            place = 2 * step + part
            total_sum += source[place] - (slab_sum(values, place) - 6.0 * values[place])
        sums[pl.ds(pl.multiple_of(step * 32, 32), 32), :] = total_sum
        return carry

    lax.fori_loop(0, 12, defect_pair, 0, unroll=2)
    halves[...] = dot(sums[...], pair_z[...])
    one[...] = (halves[pl.ds(0, 256, stride=2), :] + halves[pl.ds(1, 256, stride=2), :]).reshape(16, 16, 128)
    one_x[...] = one[:8]
    one_y[...] = one[:, :8]
    columns = dot(ends_one[...], one[...].reshape(256, 128), ((1,), (1,)))
    one_head[...] = columns[:8]
    one_tail[...] = columns[8:]

    plane = parity_plane((16, 128))
    for place in range(16):
        swept[place] = jnp.where(plane == (place & 1), one[place] * (-4.0 * SIXTH), 0.0)
    relax(swept, lambda place: one[place], 4.0, 1, 0, 16)
    for step in range(8):
        total_sum = jnp.zeros((16, 128), jnp.float32)
        for part in range(2):
            place = 2 * step + part
            total_sum += one[place] - (slab_sum(swept, place) - 6.0 * swept[place]) * 0.25
        rows[8 * step : 8 * step + 8, :] = total_sum[:8]
    packed = jnp.zeros((8, 128), jnp.float32)
    for part in range(4):
        both = rows[pl.ds(2 * part, 8, stride=8), :] + rows[pl.ds(2 * part + 1, 8, stride=8), :]
        packed += dot(both, pair_two[128 * part : 128 * part + 128, :])

    def measure_slab(place, carry):
        mass, speed = carry
        density = conserved[0, place]
        inverse = 1.0 / density
        first, second, third = conserved[1, place], conserved[2, place], conserved[3, place]
        kinetic = 0.5 * inverse * (first * first + second * second + third * third)
        pressure = (gamma_gas - 1.0) * (conserved[4, place] - kinetic)
        signal = (jnp.abs(first) + jnp.abs(second) + jnp.abs(third)) * inverse
        signal += 3.0 * jnp.sqrt(gamma_gas * pressure * inverse)
        return mass + density, jnp.maximum(speed, signal)

    blank = jnp.zeros((16, 128), jnp.float32)
    mass, speed = lax.fori_loop(0, extent, measure_slab, (blank, blank), unroll=8)
    mass = jnp.sum(jnp.sum(mass, axis=0, keepdims=True), axis=1, keepdims=True)
    speed = jnp.max(jnp.max(speed, axis=0, keepdims=True), axis=1, keepdims=True)
    lane = lax.broadcasted_iota(jnp.int32, (1, 128), 1)
    extra = jnp.where(lane == 0, mass, jnp.where(lane == 1, speed, 0.0))
    count = payload.shape[0] // 5
    for part in range(4):
        payload[pl.ds(part, count, stride=5), :] = jnp.broadcast_to(packed[part : part + 1], (count, 128))
    payload[pl.ds(4, count, stride=5), :] = jnp.broadcast_to(extra, (count, 128))
    source_copy.wait()
    values_copy.wait()


def cas(extent):
    angle = 2.0 * np.pi / extent * np.outer(np.arange(extent), np.arange(extent))
    return (np.cos(angle) + np.sin(angle)) / np.sqrt(extent)


def eigen(extent, spacing_sq):
    return (2.0 * np.cos(2.0 * np.pi / extent * np.arange(extent)) - 2.0) / spacing_sq


def coarse_tables(planes, groups, spacing_sq):
    half = planes // 2
    line = cas(128)
    same = np.repeat(np.eye(2), 2, 0)
    spread = np.repeat(line, 2, 0).reshape(8, 32, 128)
    forward = np.einsum("ab,gzk->gazbk", same, spread).reshape(1024, 256)
    across = cas(2 * groups).reshape(2 * groups, groups, 2)
    plane = np.einsum("px,qgb->pqbxg", cas(half), across).reshape(2 * groups * half, 2 * groups * half)
    total = (eigen(half, spacing_sq)[:, None] + eigen(2 * groups, spacing_sq)).reshape(-1, 1) + eigen(128, spacing_sq)
    total[0, 0] = 1.0
    inverse = 1.0 / total
    inverse[0, 0] = 0.0
    tables = (0.125 * forward, plane, inverse, plane.T, forward.T)
    return tuple(np.ascontiguousarray(table, dtype=np.float32) for table in tables)


def pick_table():
    table = np.zeros((3, 4, 32, 4, 128), np.float32)
    for line in range(4):
        for cell in range(32):
            table[0, line, cell, line, 2 * cell : 2 * cell + 2] = 1.0
        for cell in range(2):
            table[1, line, cell, line, 64 + 2 * cell : 66 + 2 * cell] = 1.0
            table[2, line, 30 + cell, line, 124 + 2 * cell : 126 + 2 * cell] = 1.0
    return table.reshape(384, 512)


def post_kernel(
    planes, groups, cells_total,
    where_ref, gathered, values, source, one_own, x_left, x_right, y_left, y_right, z_left, z_right, conserved, update,
    to_line, to_plane, inverse, from_plane, from_line, pick, place_one, refine_z,
    updated, potential_out,
    coarse, rhs, stage, chosen, extra, one_rhs, one, fine_low, fine_high, work,
    *held,
):
    far = (to_line, to_plane, inverse, from_plane, from_line, pick, one_own, x_left, x_right, y_left, y_right, z_left, z_right)
    far += (place_one, refine_z, values, source, conserved, update)
    arrivals = held[-1]
    copies = [pltpu.make_async_copy(ref, near, arrivals.at[number]) for number, (ref, near) in enumerate(zip(far, held))]
    for copy in copies:
        copy.start()
    to_line, to_plane, inverse, from_plane, from_line, pick, one_own, x_left, x_right, y_left, y_right, z_left, z_right = held[:13]
    place_one, refine_z, values, source, conserved, update = held[13:-1]

    last = gathered[pl.ds(4, gathered.shape[0] // 5, stride=5), :]
    lane_row = lax.broadcasted_iota(jnp.int32, (1, 128), 1)
    mass = jnp.sum(jnp.where(lane_row == 0, jnp.sum(last, axis=0, keepdims=True), 0.0), axis=1, keepdims=True)
    speed = jnp.sum(jnp.where(lane_row == 1, jnp.max(last, axis=0, keepdims=True), 0.0), axis=1, keepdims=True)
    offset = mass * (-coupling / cells_total)
    step_size = courant / speed

    spacing_sq = 16.0
    lane = lax.broadcasted_iota(jnp.int32, (8, 128), 1)
    cell = lane & 31
    plane = (cell + (lane >> 5)) & 1

    def tile(place, group):
        return pl.ds(pl.multiple_of((place * groups + group) * 8, 8), 8)

    def tile_sum(place, group):
        centre = coarse[tile(place, group), :]
        total_sum = coarse[tile(lax.rem(place + 1, planes), group), :]
        total_sum += coarse[tile(lax.rem(place + planes - 1, planes), group), :]
        after = coarse[tile(place, (group + 1) % groups), :]
        before = coarse[tile(place, (group + groups - 1) % groups), :]
        total_sum += turn(jnp.where(lane < 32, after, centre), -32, 1)
        total_sum += turn(jnp.where(lane >= 96, before, centre), 32, 1)
        total_sum += jnp.where(cell == 31, turn(turn(centre, -1, 0), 31, 1), turn(centre, -1, 1))
        total_sum += jnp.where(cell == 0, turn(turn(centre, 1, 0), -31, 1), turn(centre, 1, 1))
        return centre, total_sum

    def coarse_relax(colour):
        def body(step, carry):
            tiles = [(4 * step + part, group) for part in range(4) for group in range(groups)]
            fresh = []
            for place, group in tiles:
                centre, total_sum = tile_sum(place, group)
                renewed = (total_sum - spacing_sq * rhs[tile(place, group), :]) * SIXTH
                fresh.append(jnp.where(plane == ((colour + place) & 1), renewed, centre))
            for (place, group), cells in zip(tiles, fresh):
                coarse[tile(place, group), :] = cells
            return carry

        lax.fori_loop(0, planes // 4, body, 0)

    for place in range(planes):
        for group in range(groups):
            first_row = ((place // 4) * groups + group) * 8
            cells = gathered[pl.ds(5 * first_row + place % 4, 8, stride=5), :] + offset
            here = pl.ds((place * groups + group) * 8, 8)
            rhs[here, :] = cells
            coarse[here, :] = jnp.where(plane == (place & 1), cells * (-spacing_sq * SIXTH), 0.0)
    coarse_relax(1)

    def defect_pair(step, carry):
        for group in range(groups):
            total = jnp.zeros((8, 128), jnp.float32)
            for part in range(2):
                place = 2 * step + part
                centre, total_sum = tile_sum(place, group)
                total += rhs[tile(place, group), :] - (total_sum - 6.0 * centre) * (1.0 / spacing_sq)
            stage[tile(step, group), :] = total
        return carry

    half = planes // 2
    lines = half * groups
    for copy in copies[:5]:
        copy.wait()
    lax.fori_loop(0, half, defect_pair, 0, unroll=2)
    modes = jnp.zeros((lines, 256), jnp.float32)
    for part in range(8):
        modes += dot(stage[pl.ds(part, lines, stride=8), :], to_line[128 * part : 128 * part + 128, :])
    modes = jnp.concatenate([modes[:, :128], modes[:, 128:]], 0)
    modes = dot(from_plane[...], dot(to_plane[...], modes) * inverse[...])
    modes = jnp.concatenate([modes[:lines], modes[lines:]], 1)
    for part in range(8):
        stage[pl.ds(part, lines, stride=8), :] = dot(modes, from_line[:, 128 * part : 128 * part + 128])

    def add_back(step, carry):
        for group in range(groups):
            correction = stage[tile(step, group), :]
            for part in range(2):
                coarse[tile(2 * step + part, group), :] += correction
        return carry

    lax.fori_loop(0, half, add_back, 0, unroll=2)
    coarse_relax(0)
    coarse_relax(1)

    my_x, my_y, my_z = where_ref[0], where_ref[1], where_ref[2]
    for number, along_y in enumerate((0, 1, groups - 1)):
        for row, along_x in enumerate((0, 1, 2, 3, 4, 5, planes - 2, planes - 1)):
            for column, along_z in enumerate((0, 1, 7)):
                place = lax.rem(4 * my_x + along_x, planes)
                group = lax.rem(my_y + along_y, groups)
                line = lax.rem(my_z + along_z, 8)
                chosen[8 * number + row : 8 * number + row + 1, 128 * column : 128 * column + 128] = coarse[
                    pl.ds((place * groups + group) * 8 + line, 1), :
                ]
    for copy in copies[5:15]:
        copy.wait()
    picked = dot(chosen[...], pick[...])
    for number, line, slot in ((0, 0, 0), (0, 1, 2), (0, 2, 4), (0, 3, 6), (1, 0, 8), (1, 1, 10), (2, 2, 20), (2, 3, 22)):
        rows = picked[8 * number : 8 * number + 8, 128 * line : 128 * line + 128]
        for part in range(2):
            for twice in range(2):
                extra[pl.ds(24 * part + slot + twice, 8, stride=48), :] = rows

    sides = jnp.concatenate([z_right[...], z_left[...]], 0)
    beside = dot(sides, place_one[...], ((0,), (0,))).reshape(16, 16, 128)
    line_one = lax.broadcasted_iota(jnp.int32, (24, 128), 0)
    lane_one = lax.broadcasted_iota(jnp.int32, (24, 128), 1)
    plane_one = (line_one + lane_one) & 1
    from_z = jnp.logical_and(lane_one >= 64, jnp.logical_or(line_one < 10, line_one >= 22))
    for place in range(24):
        if place < 10 or place >= 22:
            row = place if place < 10 else place - 8
            cells = jnp.concatenate([one_own[row, :8], y_right[row], y_left[row]], 0)
            sideways = beside[row]
            cells = jnp.where(from_z, jnp.concatenate([sideways, sideways[8:]], 0), cells)
        elif place < 13 or place >= 19:
            cells = x_right[place - 8] if place < 13 else x_left[place - 16]
            cells = jnp.concatenate([cells, cells[8:]], 0)
        else:
            cells = jnp.zeros((24, 128), jnp.float32)
        cells = cells + offset
        one_rhs[place] = cells
        one[place] = jnp.where(plane_one == (place & 1), cells * (-4.0 * SIXTH), 0.0)
    relax(one, lambda place: one_rhs[place], 4.0, 1, -4, 16)
    for row in range(16):
        place = row if row < 12 else row + 8
        one[place] += extra[24 * row : 24 * row + 24, :]
    relax(one, lambda place: one_rhs[place], 4.0, 0, -3, 14)
    relax(one, lambda place: one_rhs[place], 4.0, 1, -2, 12)

    wide = jnp.concatenate([one[0:10], one[22:24]], 0).reshape(288, 128)
    wide = dot(wide, refine_z[...])
    for row in range(12):
        for part, fine in ((0, fine_low), (1, fine_high)):
            cells = wide[24 * row : 24 * row + 24, 128 * part : 128 * part + 128]
            for twice in range(2):
                fine[pl.ds(32 * row + twice, 8, stride=2), :] = cells[:8]
                fine[pl.ds(32 * row + 16 + twice, 4, stride=2), :] = cells[8:12]
                fine[pl.ds(32 * row + 24 + twice, 4, stride=2), :] = cells[20:24]
    plane_fine = parity_plane((32, 256))
    for copy in copies[15:]:
        copy.wait()
    for place in tuple(range(20)) + tuple(range(28, 32)):
        row = place // 2 if place < 20 else place // 2 - 4
        lift = jnp.concatenate([fine_low[32 * row : 32 * row + 32, :], fine_high[32 * row : 32 * row + 32, :]], 1)
        moved = jnp.where(plane_fine == (place & 1), offset * (-SIXTH), offset * (-2.0 * SIXTH))
        work[place] = values[place] + (lift + moved)
    extent = potential_out.shape[0]
    relax(work, lambda place: source[place] + offset, 1.0, 0, -2, extent + 4)
    relax(work, lambda place: source[place] + offset, 1.0, 1, -1, extent + 2)

    def finish(place, carry):
        cells = work[place]
        after, before = work[lax.rem(place + 1, 32)], work[lax.rem(place + 31, 32)]
        along_x = (after[:16, :128] - before[:16, :128]) * 0.5
        along_y = ((turn(cells, -1, 0) - turn(cells, 1, 0)) * 0.5)[:16, :128]
        along_z = ((turn(cells, -1, 1) - turn(cells, 1, 1)) * 0.5)[:16, :128]
        potential_out[place] = cells[:16, :128]
        density = conserved[0, place]
        first, second, third = conserved[1, place], conserved[2, place], conserved[3, place]
        energy_source = first * along_x + second * along_y + third * along_z
        updated[0, place] = density + step_size * update[0, place]
        updated[1, place] = first + step_size * (update[1, place] - density * along_x)
        updated[2, place] = second + step_size * (update[2, place] - density * along_y)
        updated[3, place] = third + step_size * (update[3, place] - density * along_z)
        updated[4, place] = conserved[4, place] + step_size * (update[4, place] - energy_source)
        return carry

    lax.fori_loop(0, extent, finish, 0, unroll=4)


def flux_x_kernel(fluid, left, right, out, states, fluxes):
    extent = fluid.shape[1]

    def fill(place, cells):
        for member, values in enumerate(primitives(*cells)):
            states[place, member] = values

    for row in range(2):
        for place, arrived, at in ((row, left, 2 * WIDE - 2 + row), (extent + 2 + row, right, WIDE + row)):
            fill(place, [arrived[at]] + [arrived[2 * WIDE + 2 * part + row] for part in range(4)])

    def own(place, carry):
        fill(place + 2, [fluid[member, place] for member in range(5)])
        return carry

    def face(place, carry):
        around = [[states[place + step, member] for member in range(5)] for step in range(4)]
        for member, values in enumerate(face_flux(*around, 0)):
            fluxes[place, member] = values
        return carry

    def difference(place, carry):
        for member in range(5):
            out[member, place] = fluxes[place, member] - fluxes[place + 1, member]
        return carry

    lax.fori_loop(0, extent, own, 0, unroll=2)
    lax.fori_loop(0, extent + 1, face, 0)
    lax.fori_loop(0, extent, difference, 0)


def flux_y_kernel(fluid, left, right, part, out, beside):
    extent = fluid.shape[1]
    lines = extent + 2 * WIDE
    row = lax.broadcasted_iota(jnp.int32, (8, 128), 0)
    for member in range(4):
        for line in range(2):
            place = 2 * lines + 2 * (2 * member + line)
            beside.at[member][pl.ds(line, extent, stride=8), :] = right[place : place + 2].reshape(16, 128)
            beside.at[member][pl.ds(6 + line, extent, stride=8), :] = left[place : place + 2].reshape(16, 128)

    def slab(place, carry):
        far = jnp.where(row < 4, right[lines + place], left[lines + place])
        cells = [jnp.concatenate([fluid[0, place], far], 0)]
        for member in range(4):
            far = beside[member, pl.ds(pl.multiple_of(8 * place, 8), 8), :]
            cells.append(jnp.concatenate([fluid[1 + member, place], far], 0))
        state = primitives(*cells)
        around = [[turn(values, -step, 0) for values in state] for step in (-1, 0, 1, 2)]
        for member, values in enumerate(face_flux(around[0], state, around[2], around[3], 1)):
            out[member, place] = part[member, place] + (turn(values, 1, 0) - values)[:16]
        return carry

    lax.fori_loop(0, extent, slab, 0)


def flux_z_kernel(fluid, left, right, ends, part, out, thin, beside):
    extent = fluid.shape[1]
    lines = extent + 2 * WIDE
    for start, count, ref in ((32 * lines, 32 * extent, thin), (64 * lines, 64 * extent, beside)):
        sides = jnp.concatenate([right[:, start : start + count], left[:, start : start + count]], 0)
        ref[...] = dot(sides, ends[...], ((0,), (0,)))

    def slab(place, carry):
        far = thin[pl.ds(pl.multiple_of(32 * place, 32), 16), :]
        cells = [jnp.concatenate([fluid[0, place], far], 1)]
        for member in range(4):
            far = beside[pl.ds(pl.multiple_of(16 * extent * member + 16 * place, 16), 16), :]
            cells.append(jnp.concatenate([fluid[1 + member, place], far], 1))
        state = primitives(*cells)
        around = [[turn(values, -step, 1) for values in state] for step in (-1, 0, 1, 2)]
        for member, values in enumerate(face_flux(around[0], state, around[2], around[3], 2)):
            out[member, place] = part[member, place] + (turn(values, 1, 1) - values)[:, :128]
        return carry

    lax.fori_loop(0, extent, slab, 0)


def call(kernel, shapes, scratch=(), operands=None, late=0):
    extra = {}
    if late:
        results = [pl.BlockSpec(memory_space=pl.ANY if number < late else pltpu.VMEM) for number in range(len(shapes))]
        extra = dict(out_specs=results)
    if operands is not None:
        specs = [pl.BlockSpec(shape, functools.partial(lambda rank, step: (0,) * rank, len(shape))) for shape in operands]
        results = [pl.BlockSpec(shape, functools.partial(lambda rank, step: (0,) * rank, len(shape))) for shape in shapes]
        extra = dict(grid=(1,), in_specs=specs, out_specs=results)
    return pl.pallas_call(
        kernel,
        **extra,
        out_shape=[jax.ShapeDtypeStruct(shape, jnp.float32) for shape in shapes],
        scratch_shapes=[pltpu.VMEM(shape, jnp.float32) for shape in scratch]
        + ([pltpu.SemaphoreType.DMA((late,))] if late else []),
        compiler_params=PRE if late else SMALL,
    )


def halved(fine):
    return np.repeat(np.eye(fine // 2, dtype=np.float32), 2, 0)


def shards(conserved, potential):
    cells_x, cells_y, cells_z = potential.shape
    count_x, count_y, count_z = (lax.axis_size(axis) for axis in AXES)
    devices = count_x * count_y * count_z
    lines = cells_x + 2 * WIDE
    block, whole, flat = (cells_x, cells_y, cells_z), conserved.shape, (5, cells_x * cells_y, cells_z)
    side, slab, ends = (2 * WIDE + 8, cells_y, cells_z), (2 * lines + 16, 8, cells_z), end_columns(cells_z, WIDE)
    fluid_rows = conserved.reshape(flat)

    head, tail = call(pack_x_kernel, [side] * 2, (), [block, whole])(potential, conserved)
    x_left, x_right = shift(tail, "gx", 1), shift(head, "gx", -1)
    head, tail = call(pack_y_kernel, [slab] * 2, (), [block, (1,) + block, flat, side, side])(
        potential, conserved, fluid_rows, x_left, x_right
    )
    y_left, y_right = shift(tail, "gy", 1), shift(head, "gy", -1)
    fluid, *sides, head, tail = lax.optimization_barrier((conserved, x_left, x_right, head, tail))
    update = call(flux_x_kernel, [whole], [(cells_x + 4, 5) + block[1:], (cells_x + 1, 5) + block[1:]])(fluid, *sides)[0]
    y_left, y_right, update = lax.optimization_barrier((y_left, y_right, update))
    columns = (8, 64 * lines + 4 * cells_x * cells_y)
    main, head, tail = call(
        pack_z_kernel,
        [(2 * lines, 32, cells_z), columns, columns],
        (),
        [block, (1,) + block, flat, side, side, slab, slab, ends.shape],
    )(potential, conserved, fluid_rows, x_left, x_right, y_left, y_right, ends)
    z_left, z_right = shift(tail, "gz", 1), shift(head, "gz", -1)
    fluid, *sides, update, head = lax.optimization_barrier((conserved, y_left, y_right, update, head))
    update = call(flux_y_kernel, [whole], [(4, 8 * cells_x, cells_z)])(fluid, *sides, update)[0]
    z_left, z_right, update = lax.optimization_barrier((z_left, z_right, update))

    pair_two = np.zeros((4, 128, 4, 32), np.float32)
    for part in range(4):
        pair_two[part, :64, part] = 0.125 * halved(64)
    window = (32, 32, 2 * cells_z)
    sizes = [window, window, (16, 16, 128), (8, 16, 128), (16, 8, 128), (8, 256), (8, 256), (devices * 5, 128)]
    tables = (0.125 * halved(256), pair_two.reshape(512, 128))
    values, source, one, one_x, one_y, one_head, one_tail, payload = call(
        pre_kernel,
        sizes,
        [window, window, (512, 256), (512, 128), (16, 16, 128), (64, 128)],
        late=2,
    )(main, z_left, z_right, ends, end_columns(64, 5), conserved, *tables)

    one_halo = [shift(one_x, "gx", 1), shift(one_x, "gx", -1), shift(one_y, "gy", 1), shift(one_y, "gy", -1)]
    one_halo.append(shift(one_tail, "gz", 1))
    gathered = lax.all_to_all(payload.reshape(devices, 1, 640), AXES, 0, 0, tiled=True).reshape(devices * 5, 128)

    fluid, update, *sides, _ = lax.optimization_barrier((conserved, update, z_left, z_right, payload))
    update = call(flux_z_kernel, [whole], [(32 * cells_x, cells_z), (64 * cells_x, cells_z)])(fluid, *sides, ends, update)[0]
    one_head, update = lax.optimization_barrier((one_head, update))
    one_halo.append(shift(one_head, "gz", -1))
    planes, groups = 4 * count_x, count_y
    position = jnp.stack([lax.axis_index(axis) for axis in AXES]).astype(jnp.int32)
    operands = (gathered, values, source, one, *one_halo, conserved, update)
    operands += coarse_tables(planes, groups, 64.0) + (pick_table(), place_columns(64, 5), halved(256).T)
    order = (12, 13, 14, 15, 16, 17, 3, 4, 5, 6, 7, 8, 9, 18, 19, 1, 2, 10, 11)
    tiles = planes * groups * 8
    updated, potential_out = pl.pallas_call(
        functools.partial(post_kernel, planes, groups, float(devices * cells_x * cells_y * cells_z)),
        out_shape=[jax.ShapeDtypeStruct(array.shape, jnp.float32) for array in (conserved, potential)],
        in_specs=[pl.BlockSpec(memory_space=pltpu.SMEM)]
        + [pl.BlockSpec(memory_space=pl.ANY if number else pltpu.VMEM) for number in range(len(operands))],
        scratch_shapes=[
            pltpu.VMEM(shape, jnp.float32)
            for shape in (
                (tiles + 8, 128), (tiles, 128), (tiles // 2, 128), (24, 384), (384, 128),
                (24, 24, 128), (24, 24, 128), (400, 128), (400, 128), (32, 32, 256),
            )
        ]
        + [pltpu.VMEM(operands[number].shape, jnp.float32) for number in order]
        + [pltpu.SemaphoreType.DMA((len(order),))],
        compiler_params=BIG,
    )(position, *operands)
    return (updated, potential_out)


def solution(mesh):
    in_specs = (P(None, "gx", "gy", "gz"), P("gx", "gy", "gz"))
    out_specs = (P(None, "gx", "gy", "gz"), P("gx", "gy", "gz"))
    return jax.shard_map(shards, mesh=mesh, in_specs=in_specs, out_specs=out_specs, check_vma=False)
```
